32 devices in a mesh: grp: 2 (over y), lat: 4 (over z), lon: 2 (over x), role: 2 (over core).
Axes of the slice: x: 2, y: 2, z: 4, core: 2. Of those that a mesh axis runs over, the one named last changes fastest.
Arguments:
- eastern_edge_current: float32 [8, 128, 256], P('lon', ('grp', 'lat', 'role')), parts along dimension 1, may hold values from -1.5 to 1.5
- northern_edge_current: float32 [8, 128, 256], P('lon', ('grp', 'lat', 'role')), parts along dimension 1, may hold values from -1.5 to 1.5
- thermal_anomaly: float32 [8, 128, 256], P('lon', ('grp', 'lat', 'role')), parts along dimension 1, may hold values from -6 to 6
- prior_warming: float32 [8, 128, 256], P('lon', ('grp', 'lat', 'role')), parts along dimension 1, may hold values from 0 to 0.5
- solute_fields: float32 [24, 8, 128, 256], P(None, None, ('grp', 'lat', 'role'), 'lon'), parts along dimension 2, may hold values from -6 to 6
- submerged_layer_count: int32 [128, 256], P(('grp', 'lat', 'role')), parts along dimension 0, may hold values from 0 to 8
- reaction_rates: float32 [24, 24], replicated, may hold values from -1.25 to 1.25
Outputs:
- u_out: float32 [8, 128, 256], P('lon', ('grp', 'lat', 'role')), parts along dimension 1
- v_out: float32 [8, 128, 256], P('lon', ('grp', 'lat', 'role')), parts along dimension 1
- temp_out: float32 [8, 128, 256], P('lon', ('grp', 'lat', 'role')), parts along dimension 1
- heating_out: float32 [8, 128, 256], P('lon', ('grp', 'lat', 'role')), parts along dimension 1
- tracers_out: float32 [24, 8, 128, 256], P(None, None, ('grp', 'lat', 'role'), 'lon'), parts along dimension 2
The draws below stay inside these ranges and needn't reach their ends.
There are 2 independent parts, one for each index of `grp`. The reference program is written for one: setup_inputs(seed, part) draws one part's arguments, and reference() takes and returns one part's arrays. A program takes and returns all parts, laid end to end along the dimension named above; an argument that names none is the same for every part. Nothing has to cross between parts.
All inputs are finite; a program needn't handle non-finite values.
Results may differ from the reference program's by a relative error of at most 0.0001.
Values sent between devices are 32-bit elements; how exact they have to be, the bound alone decides.
A program may use at most 64 MiB of HBM per device.

```python
import jax
import jax.numpy as jnp
from jax import lax

TR = 24
DEPTH_LAYERS = 8
STEPS = 2
GRID_PARALLELS = 64
GRID_MERIDIANS = 256


def place_ends(array, key, low, high):
    longest = array.shape.index(max(array.shape))
    spots = []
    for shift in (0, 1):
        where = [jax.random.randint(jax.random.fold_in(key, axis), (), 0, length) for axis, length in enumerate(array.shape)]
        where[longest] = (where[longest] + shift) % array.shape[longest]
        spots.append(tuple(where))
    return array.at[spots[0]].set(low).at[spots[1]].set(high)


def shard_levels(key, shape, shards, low, high):
    level, own = 1.0, jax.random.fold_in(key, 6)
    for position, parts in shards:
        steps = jnp.exp(jax.random.uniform(jax.random.fold_in(own, position), (parts,), jnp.float32, low / len(shards), high / len(shards)))
        level = level * jnp.repeat(steps, shape[position] // parts).reshape([-1 if axis == position else 1 for axis in range(len(shape))])
    return level


def scatter_about(rng, extent, spread, limit, split=(), kind=jnp.bfloat16):
    values = jax.random.normal(rng, extent, jnp.float32) * spread
    if len(split) > 0:
        values = shard_levels(rng, extent, split, -0.22, 0.18) * values
    return jnp.clip(values, min=-limit, max=limit).astype(kind)


def setup_inputs(seed: int = 0, part: int = 0) -> dict:
    key_list = jax.random.split(jax.random.key(seed), 8)
    part_keys = jax.random.split(jax.random.fold_in(key_list[7], part), 8)
    return {
        "eastern_edge_current": scatter_about(part_keys[0], (DEPTH_LAYERS, GRID_PARALLELS, GRID_MERIDIANS), 0.3, 1.5, ((0, 2), (1, 8)), jnp.float32),
        "northern_edge_current": scatter_about(part_keys[1], (DEPTH_LAYERS, GRID_PARALLELS, GRID_MERIDIANS), 0.3, 1.5, ((0, 2), (1, 8)), jnp.float32),
        "thermal_anomaly": scatter_about(part_keys[2], (DEPTH_LAYERS, GRID_PARALLELS, GRID_MERIDIANS), 1.0, 6.0, ((0, 2), (1, 8)), jnp.float32),
        "prior_warming": jnp.clip(0.5 * jax.random.uniform(part_keys[3], (DEPTH_LAYERS, GRID_PARALLELS, GRID_MERIDIANS), jnp.float32) ** shard_levels(part_keys[3], (DEPTH_LAYERS, GRID_PARALLELS, GRID_MERIDIANS), ((0, 2), (1, 8)), -0.2, 0.2), 0.0, 0.5),
        "solute_fields": scatter_about(part_keys[4], (TR, DEPTH_LAYERS, GRID_PARALLELS, GRID_MERIDIANS), 1.0, 6.0, ((2, 8), (3, 2)), jnp.float32),
        "submerged_layer_count": place_ends(jax.random.randint(part_keys[5], (GRID_PARALLELS, GRID_MERIDIANS), 0, DEPTH_LAYERS + 1), jax.random.fold_in(part_keys[5], 1), 0, DEPTH_LAYERS).astype(jnp.int32),
        "reaction_rates": scatter_about(key_list[6], (TR, TR), TR ** -0.5, 1.25, (), jnp.float32),
    }


def eastern_neighbor(q):
    return jnp.concatenate([q[..., 1:], jnp.zeros_like(q[..., :1])], axis=-1)


def west(q):
    return jnp.concatenate([jnp.zeros_like(q[..., :1]), q[..., :-1]], axis=-1)


def northern_neighbor(q):
    return jnp.concatenate([q[..., 1:, :], jnp.zeros_like(q[..., :1, :])], axis=-2)


def south(q):
    return jnp.concatenate([jnp.zeros_like(q[..., :1, :]), q[..., :-1, :]], axis=-2)


def diffusion_operator(q):
    return eastern_neighbor(q) + west(q) + northern_neighbor(q) + south(q) - 4.0 * q


def reference(eastern_edge_current, northern_edge_current, thermal_anomaly, prior_warming, solute_fields, submerged_layer_count, reaction_rates):
    levels = jnp.arange(DEPTH_LAYERS, dtype=jnp.int32)
    ocean_mask = (levels[:, None, None] < submerged_layer_count[None, :, :]).astype(jnp.float32)
    ocean_mask_eastward = ocean_mask * eastern_neighbor(ocean_mask)
    ocean_mask_poleward = ocean_mask * northern_neighbor(ocean_mask)
    coriolis_parameter = (2.0 * (jnp.arange(GRID_PARALLELS, dtype=jnp.float32) + 0.5) / GRID_PARALLELS - 1.0)[:, None]
    thermal_energy = prior_warming
    eastward_current, poleward_current, seawater_warmth, solute_amount = eastern_edge_current, northern_edge_current, thermal_anomaly, solute_fields
    for step in range(STEPS):
        updated_eastward_flow = ocean_mask_eastward * (eastward_current + 0.1 * diffusion_operator(eastward_current) + 0.3 * coriolis_parameter * poleward_current - 0.2 * (eastern_neighbor(seawater_warmth) - seawater_warmth))
        updated_poleward_flow = ocean_mask_poleward * (poleward_current + 0.1 * diffusion_operator(poleward_current) - 0.3 * coriolis_parameter * eastward_current - 0.2 * (northern_neighbor(seawater_warmth) - seawater_warmth))
        seawater_warmth = ocean_mask * (seawater_warmth + 0.1 * diffusion_operator(seawater_warmth) + 0.5 * thermal_energy)
        eastward_current, poleward_current = updated_eastward_flow, updated_poleward_flow
        flux_x = jnp.maximum(eastward_current, 0.0) * solute_amount + jnp.minimum(eastward_current, 0.0) * eastern_neighbor(solute_amount)
        flux_y = jnp.maximum(poleward_current, 0.0) * solute_amount + jnp.minimum(poleward_current, 0.0) * northern_neighbor(solute_amount)
        advected = solute_amount - 0.5 * ((flux_x - west(flux_x)) + (flux_y - south(flux_y)))
        atten = 0.1 + 0.3 * jnp.maximum(advected[0], 0.0)
        summed = jnp.cumsum(atten, axis=0)
        depth_tau = jnp.concatenate([jnp.zeros_like(atten[:1]), summed[:-1]], axis=0)
        top = jnp.exp(-depth_tau)
        thermal_energy = 2.0 * ocean_mask * (top - jnp.exp(-(depth_tau + atten)))
        react = jnp.einsum("ab,bzyx->azyx", reaction_rates, advected, precision=lax.Precision.HIGHEST)
        solute_amount = ocean_mask * (advected + 0.5 * top * react)
    return eastward_current, poleward_current, seawater_warmth, thermal_energy, solute_amount
```

```python
import functools

import jax
import jax.numpy as jnp
from jax import lax
from jax.experimental import pallas as pl
from jax.experimental.pallas import tpu as pltpu
from jax.sharding import PartitionSpec as P

ROWS = 8
LANES = 128
PAD = 4
EXT = ROWS + 2 * PAD
F32 = jnp.float32


def east(q):
    lane = lax.broadcasted_iota(jnp.int32, q.shape, q.ndim - 1)
    return jnp.where(lane < q.shape[-1] - 1, pltpu.roll(q, q.shape[-1] - 1, q.ndim - 1), 0.0)


def west(q):
    lane = lax.broadcasted_iota(jnp.int32, q.shape, q.ndim - 1)
    return jnp.where(lane > 0, pltpu.roll(q, 1, q.ndim - 1), 0.0)


def north(q):
    return pltpu.roll(q, q.shape[-2] - 1, q.ndim - 2)


def south(q):
    return pltpu.roll(q, 1, q.ndim - 2)


def lap(q):
    return east(q) + west(q) + north(q) + south(q) - 4.0 * q


def kernel(
    sizes,
    u_in, v_in, t_in, h_in, c_in, n_in, r_in,
    u_out, v_out, t_out, h_out, c_out,
    pk_n, pk_s, rc_n, rc_s, cnt_n, cnt_s, ext, ext_n, t_base, wet_strip,
    c_mid, row_lo, row_hi, col_ed, got_n, got_s, got_w, got_e,
    f_send, f_recv, h_send, h_recv,
    d_ssem, d_rsem, c0_ssem, c0_rsem, c1_ssem, c1_rsem, f_ssem, f_rsem, h_ssem, h_rsem,
):
    tracers, depth, share, nlon, nrole, nstrip = sizes
    width = nlon * LANES
    s = lax.axis_index("lat") * nrole + lax.axis_index("role")
    col = lax.axis_index("lon")
    has_n, has_s = s < nstrip - 1, s > 0
    has_e, has_w = col < nlon - 1, col > 0
    sn, ss = lax.rem(s + 1, nstrip), lax.rem(s + nstrip - 1, nstrip)
    dev_n = {"lat": sn // nrole, "role": lax.rem(sn, nrole)}
    dev_s = {"lat": ss // nrole, "role": lax.rem(ss, nrole)}
    dev_e = {"lon": lax.rem(col + 1, nlon)}
    dev_w = {"lon": lax.rem(col + nlon - 1, nlon)}

    barrier = pltpu.get_barrier_semaphore()

    def greet(dev):
        pl.semaphore_signal(barrier, inc=1, device_id=dev, device_id_type=pl.DeviceIdType.MESH)

    pl.when(has_n)(lambda: greet(dev_n))
    pl.when(has_s)(lambda: greet(dev_s))
    for d in range(1, nlon):
        greet({"lon": lax.rem(col + d, nlon)})

    def copy(src, dst, ssem, rsem, dev):
        return pltpu.make_async_remote_copy(
            src_ref=src, dst_ref=dst, send_sem=ssem, recv_sem=rsem,
            device_id=dev, device_id_type=pl.DeviceIdType.MESH,
        )

    def start(copies):
        for c, send, _ in copies:
            pl.when(send)(c.start)

    def wait_recv(copies):
        for c, _, recv in copies:
            pl.when(recv)(c.wait_recv)

    def wait_send(copies):
        for c, send, _ in copies:
            pl.when(send)(c.wait_send)

    pk_n[:, 0:3, :] = v_in[:, 5:8, :]
    pk_n[:, 3:5, :] = u_in[:, 6:8, :]
    pk_n[:, 5:7, :] = t_in[:, 6:8, :]
    pk_n[:, 7:8, :] = h_in[:, 7:8, :]
    pk_s[:, 0:2, :] = u_in[:, 0:2, :]
    pk_s[:, 2:4, :] = v_in[:, 0:2, :]
    pk_s[:, 4:6, :] = t_in[:, 0:2, :]
    pk_s[:, 6:7, :] = h_in[:, 0:1, :]
    pk_s[:, 7:8, :] = h_in[:, 0:1, :]

    lane = lax.broadcasted_iota(jnp.int32, (ROWS, LANES), 1)
    row = lax.broadcasted_iota(jnp.int32, (ROWS, LANES), 0)

    def pack(m, k, x):
        row_lo[m, k] = x[:, 0, :]
        row_hi[m, k] = x[:, ROWS - 1, :]
        acc = x[0]
        for t in range(1, tracers):
            here = (lane == 2 * t - 1) | (lane == 2 * t)
            acc = jnp.where(here, pltpu.roll(x[t], 2 * t, 1), acc)
        col_ed[m, k] = acc

    for k in range(depth):
        pack(0, k, c_in[:, k])

    dyn = [
        (copy(pk_n, rc_s, d_ssem.at[0], d_rsem.at[0], dev_n), has_n, has_s),
        (copy(pk_s, rc_n, d_ssem.at[1], d_rsem.at[1], dev_s), has_s, has_n),
        (copy(n_in, cnt_s, d_ssem.at[2], d_rsem.at[2], dev_n), has_n, has_s),
        (copy(n_in, cnt_n, d_ssem.at[3], d_rsem.at[3], dev_s), has_s, has_n),
    ]
    first = [
        (copy(row_hi.at[0], got_s.at[0], c0_ssem.at[0], c0_rsem.at[0], dev_n), has_n, has_s),
        (copy(row_lo.at[0], got_n.at[0], c0_ssem.at[1], c0_rsem.at[1], dev_s), has_s, has_n),
        (copy(col_ed.at[0], got_w.at[0], c0_ssem.at[2], c0_rsem.at[2], dev_e), has_e, has_w),
        (copy(col_ed.at[0], got_e.at[0], c0_ssem.at[3], c0_rsem.at[3], dev_w), has_w, has_e),
    ]

    def second(k):
        return [
            (copy(row_hi.at[1, k], got_s.at[1, k], c1_ssem.at[0, k], c1_rsem.at[0, k], dev_n), has_n, has_s),
            (copy(row_lo.at[1, k], got_n.at[1, k], c1_ssem.at[1, k], c1_rsem.at[1, k], dev_s), has_s, has_n),
            (copy(col_ed.at[1, k], got_w.at[1, k], c1_ssem.at[2, k], c1_rsem.at[2, k], dev_e), has_e, has_w),
            (copy(col_ed.at[1, k], got_e.at[1, k], c1_ssem.at[3, k], c1_rsem.at[3, k], dev_w), has_w, has_e),
        ]

    def faces(m):
        out = []
        for d in range(1, nlon):
            p = lax.rem(col + d, nlon)
            out.append(copy(f_send.at[m, p], f_recv.at[m, col], f_ssem.at[m, d], f_rsem.at[m, d], {"lon": p}))
        return out

    def heats(m):
        out = []
        for d in range(1, nlon):
            p = lax.rem(col + d, nlon)
            out.append(copy(h_send.at[m, p], h_recv.at[m, col], h_ssem.at[m, d], h_rsem.at[m, d], {"lon": p}))
        return out

    pl.semaphore_wait(barrier, nlon - 1 + jnp.minimum(s, 1) + jnp.minimum(nstrip - 1 - s, 1))
    start(dyn)
    start(first)

    @pl.when(jnp.logical_not(has_s))
    def _():
        rc_s[...] = jnp.zeros_like(rc_s)
        cnt_s[...] = jnp.zeros_like(cnt_s)
        got_s[...] = jnp.zeros_like(got_s)

    @pl.when(jnp.logical_not(has_n))
    def _():
        rc_n[...] = jnp.zeros_like(rc_n)
        cnt_n[...] = jnp.zeros_like(cnt_n)
        got_n[...] = jnp.zeros_like(got_n)

    @pl.when(jnp.logical_not(has_w))
    def _():
        got_w[...] = jnp.zeros_like(got_w)

    @pl.when(jnp.logical_not(has_e))
    def _():
        got_e[...] = jnp.zeros_like(got_e)

    wide = tracers * ROWS
    spread = (
        lax.broadcasted_iota(jnp.int32, (wide, tracers), 0) // ROWS
        == lax.broadcasted_iota(jnp.int32, (wide, tracers), 1)
    ).astype(F32)
    gather = (
        lax.broadcasted_iota(jnp.int32, (tracers, wide), 1) // ROWS
        == lax.broadcasted_iota(jnp.int32, (tracers, wide), 0)
    ).astype(F32)
    exact = lax.Precision.HIGHEST
    rates = jnp.dot(
        spread, jnp.dot(r_in[...], gather, precision=exact, preferred_element_type=F32),
        precision=exact, preferred_element_type=F32,
    )
    same_row = (
        lax.broadcasted_iota(jnp.int32, (wide, wide), 0) % ROWS
        == lax.broadcasted_iota(jnp.int32, (wide, wide), 1) % ROWS
    )
    rates = jnp.where(same_row, rates, 0.0)
    rates_hi = rates.astype(jnp.bfloat16)
    rates_lo = (rates - rates_hi.astype(F32)).astype(jnp.bfloat16)

    zero = jnp.zeros((share, PAD, width), F32)
    for f in range(4):
        ext[f, :, 0:PAD, :] = zero
        ext[f, :, PAD + ROWS :, :] = zero
    ext_n[0:PAD, :] = jnp.zeros((PAD, width), jnp.int32)
    ext_n[PAD + ROWS :, :] = jnp.zeros((PAD, width), jnp.int32)
    for f, ref in enumerate((u_in, v_in, t_in, h_in)):
        ext[f, :, PAD : PAD + ROWS, :] = ref[...]
    ext_n[PAD : PAD + ROWS, :] = n_in[...]

    wait_recv(dyn)
    ext[0, :, 2:4, :] = rc_s[:, 3:5, :]
    ext[1, :, 1:4, :] = rc_s[:, 0:3, :]
    ext[2, :, 2:4, :] = rc_s[:, 5:7, :]
    ext[3, :, 3:4, :] = rc_s[:, 7:8, :]
    ext[0, :, 12:14, :] = rc_n[:, 0:2, :]
    ext[1, :, 12:14, :] = rc_n[:, 2:4, :]
    ext[2, :, 12:14, :] = rc_n[:, 4:6, :]
    ext[3, :, 12:13, :] = rc_n[:, 6:7, :]
    ext_n[2:4, :] = cnt_s[6:8, :]
    ext_n[12:14, :] = cnt_n[0:2, :]

    shape = (share, EXT, width)
    level = col * share + lax.broadcasted_iota(jnp.int32, shape, 0)
    wet = (level < ext_n[...][None]).astype(F32)
    wet_u = wet * east(wet)
    wet_v = wet * north(wet)
    spot = (s * ROWS - PAD + lax.broadcasted_iota(jnp.int32, shape, 1)).astype(F32)
    fcor = 0.3 * (2.0 * (spot + 0.5) / (nstrip * ROWS) - 1.0)

    def advance(u, v, t):
        new_u = wet_u * (u + 0.1 * lap(u) + fcor * v - 0.2 * (east(t) - t))
        new_v = wet_v * (v + 0.1 * lap(v) - fcor * u - 0.2 * (north(t) - t))
        return new_u, new_v

    def publish(m, u, v):
        for p in range(nlon):
            lo = p * LANES
            cols = slice(lo, lo + LANES)
            v_edge = jnp.zeros((ROWS, LANES), F32)
            u_edge = jnp.zeros((ROWS, LANES), F32)
            for l in range(share):
                f_send[m, p, l] = u[l, PAD : PAD + ROWS, cols]
                f_send[m, p, share + l] = v[l, PAD : PAD + ROWS, cols]
                v_edge = jnp.where(row == l, v[l, PAD - 1 : PAD, cols], v_edge)
                if p:
                    u_edge = jnp.where(lane == l, u[l, PAD : PAD + ROWS, lo - 1 : lo], u_edge)
            f_send[m, p, 2 * share] = v_edge
            f_send[m, p, 2 * share + 1] = u_edge
        for c in faces(m):
            c.start()
        f_recv[m, col] = f_send[m, col]

    u0, v0, t0 = ext[0], ext[1], ext[2]
    u1, v1 = advance(u0, v0, t0)
    publish(0, u1, v1)
    t1 = wet * (t0 + 0.1 * lap(t0) + 0.5 * ext[3])
    u2, v2 = advance(u1, v1, t1)
    publish(1, u2, v2)
    u_out[...] = u2[:, PAD : PAD + ROWS, :]
    v_out[...] = v2[:, PAD : PAD + ROWS, :]
    t_base[...] = (wet * (t1 + 0.1 * lap(t1)))[:, PAD : PAD + ROWS, :]
    wet_strip[...] = wet[:, PAD : PAD + ROWS, :]

    depth_here = n_in[:, pl.ds(pl.multiple_of(col * LANES, LANES), LANES)]

    def tile_step(m, source, target):
        tau = jnp.zeros((ROWS, LANES), F32)
        top = jnp.ones((ROWS, LANES), F32)
        for k in range(depth):
            if m:
                wait_recv(second(k))
            p, l = k // share, k % share
            u = f_recv[m, p, l]
            v = f_recv[m, p, share + l]
            v_s = jnp.where(row == 0, f_recv[m, p, 2 * share, l : l + 1, :], pltpu.roll(v, 1, 0))
            u_w = jnp.where(lane == 0, f_recv[m, p, 2 * share + 1, :, l : l + 1], pltpu.roll(u, 1, 1))
            a_e = -0.5 * jnp.minimum(u, 0.0)
            a_w = 0.5 * jnp.maximum(u_w, 0.0)
            a_n = -0.5 * jnp.minimum(v, 0.0)
            a_s = 0.5 * jnp.maximum(v_s, 0.0)
            a_0 = 1.0 - 0.5 * (
                (jnp.maximum(u, 0.0) - jnp.minimum(u_w, 0.0)) + (jnp.maximum(v, 0.0) - jnp.minimum(v_s, 0.0))
            )
            sides = jnp.where(lane % 2 == 0, pltpu.roll(got_w[m, k], 1, 1), pltpu.roll(got_e[m, k], LANES - 1, 1))
            parts = []
            for t in range(tracers):
                x = source[t, k]
                edge = pltpu.roll(sides, (LANES - 2 * t) % LANES, 1)
                x_n = jnp.where(row == ROWS - 1, got_n[m, k, t : t + 1, :], pltpu.roll(x, ROWS - 1, 0))
                x_s = jnp.where(row == 0, got_s[m, k, t : t + 1, :], pltpu.roll(x, 1, 0))
                x_e = jnp.where(lane == LANES - 1, edge, pltpu.roll(x, LANES - 1, 1))
                x_w = jnp.where(lane == 0, edge, pltpu.roll(x, 1, 1))
                parts.append(a_0 * x + (a_e * x_e + a_w * x_w) + (a_n * x_n + a_s * x_s))
            adv = jnp.concatenate(parts, axis=0)
            wet_k = (k < depth_here).astype(F32)
            tau = tau + (0.1 + 0.3 * jnp.maximum(parts[0], 0.0))
            below = jnp.exp(-tau)
            h_send[m, p, l] = 2.0 * wet_k * (top - below)
            hi = adv.astype(jnp.bfloat16)
            lo = (adv - hi.astype(F32)).astype(jnp.bfloat16)
            both = jnp.dot(rates_hi, jnp.concatenate([hi, lo], axis=1), preferred_element_type=F32)
            r = both[:, :LANES] + both[:, LANES:] + jnp.dot(rates_lo, hi, preferred_element_type=F32)
            new = wet_k * (adv.reshape(tracers, ROWS, LANES) + (0.5 * top) * r.reshape(tracers, ROWS, LANES))
            target[:, k] = new
            if m == 0:
                pack(1, k, new)
                start(second(k))
            top = below
        for c in heats(m):
            c.start()
        h_recv[m, col] = h_send[m, col]

    wait_recv(first)
    for c in faces(0):
        c.wait_recv()
    tile_step(0, c_in, c_mid)
    for c in faces(1):
        c.wait_recv()
    tile_step(1, c_mid, c_out)

    for c in heats(0):
        c.wait_recv()
    for p in range(nlon):
        cols = slice(p * LANES, (p + 1) * LANES)
        t_out[:, :, cols] = t_base[:, :, cols] + 0.5 * wet_strip[:, :, cols] * h_recv[0, p]
    wait_send(dyn)
    wait_send(first)
    for k in range(depth):
        wait_send(second(k))
    for m in range(2):
        for c in faces(m):
            c.wait_send()
        for c in heats(m):
            c.wait_send()
    for c in heats(1):
        c.wait_recv()
    for p in range(nlon):
        h_out[:, :, p * LANES : (p + 1) * LANES] = h_recv[1, p]


def shards(sizes, u, v, t, h, c, n, r):
    tracers, depth, share, nlon, _, _ = sizes
    strip = jax.ShapeDtypeStruct(u.shape, F32)
    tile = (ROWS, LANES)
    strip_buf = pltpu.VMEM(u.shape, F32)
    dma = pltpu.SemaphoreType.DMA
    vmem = pl.BlockSpec(memory_space=pltpu.VMEM)
    return pl.pallas_call(
        functools.partial(kernel, sizes),
        out_shape=(strip, strip, strip, strip, jax.ShapeDtypeStruct(c.shape, F32)),
        in_specs=[vmem] * 7,
        out_specs=(vmem,) * 5,
        scratch_shapes=[
            strip_buf, strip_buf, strip_buf, strip_buf,
            pltpu.VMEM(n.shape, jnp.int32), pltpu.VMEM(n.shape, jnp.int32),
            pltpu.VMEM((4, share, EXT, u.shape[2]), F32),
            pltpu.VMEM((EXT, u.shape[2]), jnp.int32),
            strip_buf, strip_buf,
            pltpu.VMEM(c.shape, F32),
            pltpu.VMEM((2, depth, tracers, LANES), F32),
            pltpu.VMEM((2, depth, tracers, LANES), F32),
            pltpu.VMEM((2, depth) + tile, F32),
            pltpu.VMEM((2, depth, tracers, LANES), F32),
            pltpu.VMEM((2, depth, tracers, LANES), F32),
            pltpu.VMEM((2, depth) + tile, F32),
            pltpu.VMEM((2, depth) + tile, F32),
            pltpu.VMEM((2, nlon, 2 * share + 2) + tile, F32),
            pltpu.VMEM((2, nlon, 2 * share + 2) + tile, F32),
            pltpu.VMEM((2, nlon, share) + tile, F32),
            pltpu.VMEM((2, nlon, share) + tile, F32),
            dma((4,)), dma((4,)), dma((4,)), dma((4,)),
            dma((4, depth)), dma((4, depth)),
            dma((2, nlon)), dma((2, nlon)), dma((2, nlon)), dma((2, nlon)),
        ],
        compiler_params=pltpu.CompilerParams(
            collective_id=0, has_side_effects=True, vmem_limit_bytes=32 * 1024 * 1024
        ),
    )(u, v, t, h, c, n, r)


def solution(mesh):
    nlon, nrole = mesh.shape["lon"], mesh.shape["role"]
    nstrip = mesh.shape["lat"] * nrole
    strip = P("lon", ("grp", "lat", "role"), None)
    tile = P(None, None, ("grp", "lat", "role"), "lon")

    def run(u, v, t, h, c, n, r):
        sizes = (c.shape[0], c.shape[1], u.shape[0] // nlon, nlon, nrole, nstrip)
        return jax.shard_map(
            functools.partial(shards, sizes),
            mesh=mesh,
            in_specs=(strip, strip, strip, strip, tile, P(("grp", "lat", "role"), None), P()),
            out_specs=(strip, strip, strip, strip, tile),
            check_vma=False,
        )(u, v, t, h, c, n, r)

    return run
```

```python
import functools

import jax
import jax.numpy as jnp
from jax import lax
from jax.experimental import pallas as pl
from jax.experimental.pallas import tpu as pltpu
from jax.sharding import PartitionSpec as P

ROWS = 8
LANES = 128
PAD = 4
EXT = ROWS + 2 * PAD
EARLY = 5
VMEM = 64 * 1024 * 1024
CUTS = 4
F32 = jnp.float32


def east(q):
    lane = lax.broadcasted_iota(jnp.int32, q.shape, q.ndim - 1)
    return jnp.where(lane < q.shape[-1] - 1, pltpu.roll(q, q.shape[-1] - 1, q.ndim - 1), 0.0)


def west(q):
    lane = lax.broadcasted_iota(jnp.int32, q.shape, q.ndim - 1)
    return jnp.where(lane > 0, pltpu.roll(q, 1, q.ndim - 1), 0.0)


def north(q):
    return pltpu.roll(q, q.shape[-2] - 1, q.ndim - 2)


def south(q):
    return pltpu.roll(q, 1, q.ndim - 2)


def lap(q):
    return east(q) + west(q) + north(q) + south(q) - 4.0 * q


def kernel(
    sizes,
    u_hbm, v_hbm, t_hbm, h_hbm, c_hbm, n_hbm, r_hbm,
    u_dst, v_dst, t_dst, h_dst, c_dst,
    pk_n, pk_s, rc_n, rc_s, cnt_n, cnt_s, ext, ext_n, t_base, wet_strip,
    c_mid, row_lo, row_hi, col_ed, got_n, got_s, got_w, got_e,
    f_send, f_recv, h_send, h_recv,
    u_in, v_in, t_in, h_in, c_in, n_in, r_in, in_sem,
    u_out, v_out, t_out, h_out, c_out, out_sem,
    d_ssem, d_rsem, c0_ssem, c0_rsem, c1_ssem, c1_rsem, f_ssem, f_rsem, h_ssem, h_rsem,
):
    tracers, depth, share, nlon, nrole, nstrip = sizes
    width = nlon * LANES
    arrays = (
        (u_hbm, u_in), (v_hbm, v_in), (t_hbm, t_in), (h_hbm, h_in), (n_hbm, n_in), (c_hbm, c_in), (r_hbm, r_in),
    )
    loads = [pltpu.make_async_copy(a, b, in_sem.at[i]) for i, (a, b) in enumerate(arrays)]
    for load in loads:
        load.start()
    s = lax.axis_index("lat") * nrole + lax.axis_index("role")
    col = lax.axis_index("lon")
    has_n, has_s = s < nstrip - 1, s > 0
    has_e, has_w = col < nlon - 1, col > 0
    sn, ss = lax.rem(s + 1, nstrip), lax.rem(s + nstrip - 1, nstrip)
    dev_n = {"lat": sn // nrole, "role": lax.rem(sn, nrole)}
    dev_s = {"lat": ss // nrole, "role": lax.rem(ss, nrole)}
    dev_e = {"lon": lax.rem(col + 1, nlon)}
    dev_w = {"lon": lax.rem(col + nlon - 1, nlon)}

    barrier = pltpu.get_barrier_semaphore()

    def greet(dev):
        pl.semaphore_signal(barrier, inc=1, device_id=dev, device_id_type=pl.DeviceIdType.MESH)

    pl.when(has_n)(lambda: greet(dev_n))
    pl.when(has_s)(lambda: greet(dev_s))
    for d in range(1, nlon):
        greet({"lon": lax.rem(col + d, nlon)})

    def copy(src, dst, ssem, rsem, dev):
        return pltpu.make_async_remote_copy(
            src_ref=src, dst_ref=dst, send_sem=ssem, recv_sem=rsem,
            device_id=dev, device_id_type=pl.DeviceIdType.MESH,
        )

    def start(copies):
        for c, send, _ in copies:
            pl.when(send)(c.start)

    def wait_recv(copies):
        for c, _, recv in copies:
            pl.when(recv)(c.wait_recv)

    def wait_send(copies):
        for c, send, _ in copies:
            pl.when(send)(c.wait_send)

    for load in loads[:5]:
        load.wait()
    pk_n[:, 0:3, :] = v_in[:, 5:8, :]
    pk_n[:, 3:5, :] = u_in[:, 6:8, :]
    pk_n[:, 5:7, :] = t_in[:, 6:8, :]
    pk_n[:, 7:8, :] = h_in[:, 7:8, :]
    pk_s[:, 0:2, :] = u_in[:, 0:2, :]
    pk_s[:, 2:4, :] = v_in[:, 0:2, :]
    pk_s[:, 4:6, :] = t_in[:, 0:2, :]
    pk_s[:, 6:7, :] = h_in[:, 0:1, :]
    pk_s[:, 7:8, :] = h_in[:, 0:1, :]

    lane = lax.broadcasted_iota(jnp.int32, (ROWS, LANES), 1)
    row = lax.broadcasted_iota(jnp.int32, (ROWS, LANES), 0)

    def pack(m, k, x):
        row_lo[m, k] = x[:, 0, :]
        row_hi[m, k] = x[:, ROWS - 1, :]
        acc = x[0]
        for t in range(1, tracers):
            here = (lane == 2 * t - 1) | (lane == 2 * t)
            acc = jnp.where(here, pltpu.roll(x[t], 2 * t, 1), acc)
        col_ed[m, k] = acc

    dyn = [
        (copy(pk_n, rc_s, d_ssem.at[0], d_rsem.at[0], dev_n), has_n, has_s),
        (copy(pk_s, rc_n, d_ssem.at[1], d_rsem.at[1], dev_s), has_s, has_n),
        (copy(n_in, cnt_s, d_ssem.at[2], d_rsem.at[2], dev_n), has_n, has_s),
        (copy(n_in, cnt_n, d_ssem.at[3], d_rsem.at[3], dev_s), has_s, has_n),
    ]
    first = [
        (copy(row_hi.at[0], got_s.at[0], c0_ssem.at[0], c0_rsem.at[0], dev_n), has_n, has_s),
        (copy(row_lo.at[0], got_n.at[0], c0_ssem.at[1], c0_rsem.at[1], dev_s), has_s, has_n),
        (copy(col_ed.at[0], got_w.at[0], c0_ssem.at[2], c0_rsem.at[2], dev_e), has_e, has_w),
        (copy(col_ed.at[0], got_e.at[0], c0_ssem.at[3], c0_rsem.at[3], dev_w), has_w, has_e),
    ]

    def second(k):
        return [
            (copy(row_hi.at[1, k], got_s.at[1, k], c1_ssem.at[0, k], c1_rsem.at[0, k], dev_n), has_n, has_s),
            (copy(row_lo.at[1, k], got_n.at[1, k], c1_ssem.at[1, k], c1_rsem.at[1, k], dev_s), has_s, has_n),
            (copy(col_ed.at[1, k], got_w.at[1, k], c1_ssem.at[2, k], c1_rsem.at[2, k], dev_e), has_e, has_w),
            (copy(col_ed.at[1, k], got_e.at[1, k], c1_ssem.at[3, k], c1_rsem.at[3, k], dev_w), has_w, has_e),
        ]

    def faces(m):
        out = []
        for d in range(1, nlon):
            p = lax.rem(col + d, nlon)
            out.append(copy(f_send.at[m, p], f_recv.at[m, col], f_ssem.at[m, d], f_rsem.at[m, d], {"lon": p}))
        return out

    def heats(m):
        out = []
        for d in range(1, nlon):
            p = lax.rem(col + d, nlon)
            out.append(copy(h_send.at[m, p], h_recv.at[m, col], h_ssem.at[m, d], h_rsem.at[m, d], {"lon": p}))
        return out

    pl.semaphore_wait(barrier, nlon - 1 + jnp.minimum(s, 1) + jnp.minimum(nstrip - 1 - s, 1))
    start(dyn)
    for load in loads[5:]:
        load.wait()
    for k in range(depth):
        pack(0, k, c_in[:, k])
    start(first)

    @pl.when(jnp.logical_not(has_s))
    def _():
        rc_s[...] = jnp.zeros_like(rc_s)
        cnt_s[...] = jnp.zeros_like(cnt_s)
        got_s[...] = jnp.zeros_like(got_s)

    @pl.when(jnp.logical_not(has_n))
    def _():
        rc_n[...] = jnp.zeros_like(rc_n)
        cnt_n[...] = jnp.zeros_like(cnt_n)
        got_n[...] = jnp.zeros_like(got_n)

    @pl.when(jnp.logical_not(has_w))
    def _():
        got_w[...] = jnp.zeros_like(got_w)

    @pl.when(jnp.logical_not(has_e))
    def _():
        got_e[...] = jnp.zeros_like(got_e)

    wide = tracers * ROWS
    spread = (
        lax.broadcasted_iota(jnp.int32, (wide, tracers), 0) // ROWS
        == lax.broadcasted_iota(jnp.int32, (wide, tracers), 1)
    ).astype(F32)
    gather = (
        lax.broadcasted_iota(jnp.int32, (tracers, wide), 1) // ROWS
        == lax.broadcasted_iota(jnp.int32, (tracers, wide), 0)
    ).astype(F32)
    exact = lax.Precision.HIGHEST
    rates = jnp.dot(
        spread, jnp.dot(r_in[...], gather, precision=exact, preferred_element_type=F32),
        precision=exact, preferred_element_type=F32,
    )
    same_row = (
        lax.broadcasted_iota(jnp.int32, (wide, wide), 0) % ROWS
        == lax.broadcasted_iota(jnp.int32, (wide, wide), 1) % ROWS
    )
    rates = jnp.where(same_row, rates, 0.0)
    rates_hi = rates.astype(jnp.bfloat16)
    rates_lo = (rates - rates_hi.astype(F32)).astype(jnp.bfloat16)

    zero = jnp.zeros((share, PAD, width), F32)
    for f in range(4):
        ext[f, :, 0:PAD, :] = zero
        ext[f, :, PAD + ROWS :, :] = zero
    ext_n[0:PAD, :] = jnp.zeros((PAD, width), jnp.int32)
    ext_n[PAD + ROWS :, :] = jnp.zeros((PAD, width), jnp.int32)
    for f, ref in enumerate((u_in, v_in, t_in, h_in)):
        ext[f, :, PAD : PAD + ROWS, :] = ref[...]
    ext_n[PAD : PAD + ROWS, :] = n_in[...]

    wait_recv(dyn)
    ext[0, :, 2:4, :] = rc_s[:, 3:5, :]
    ext[1, :, 1:4, :] = rc_s[:, 0:3, :]
    ext[2, :, 2:4, :] = rc_s[:, 5:7, :]
    ext[3, :, 3:4, :] = rc_s[:, 7:8, :]
    ext[0, :, 12:14, :] = rc_n[:, 0:2, :]
    ext[1, :, 12:14, :] = rc_n[:, 2:4, :]
    ext[2, :, 12:14, :] = rc_n[:, 4:6, :]
    ext[3, :, 12:13, :] = rc_n[:, 6:7, :]
    ext_n[2:4, :] = cnt_s[6:8, :]
    ext_n[12:14, :] = cnt_n[0:2, :]

    shape = (share, EXT, width)
    level = col * share + lax.broadcasted_iota(jnp.int32, shape, 0)
    wet = (level < ext_n[...][None]).astype(F32)
    wet_u = wet * east(wet)
    wet_v = wet * north(wet)
    spot = (s * ROWS - PAD + lax.broadcasted_iota(jnp.int32, shape, 1)).astype(F32)
    fcor = 0.3 * (2.0 * (spot + 0.5) / (nstrip * ROWS) - 1.0)

    def advance(u, v, t):
        new_u = wet_u * (u + 0.1 * lap(u) + fcor * v - 0.2 * (east(t) - t))
        new_v = wet_v * (v + 0.1 * lap(v) - fcor * u - 0.2 * (north(t) - t))
        return new_u, new_v

    def publish(m, u, v):
        for p in range(nlon):
            lo = p * LANES
            cols = slice(lo, lo + LANES)
            v_edge = jnp.zeros((ROWS, LANES), F32)
            u_edge = jnp.zeros((ROWS, LANES), F32)
            for l in range(share):
                f_send[m, p, l] = u[l, PAD : PAD + ROWS, cols]
                f_send[m, p, share + l] = v[l, PAD : PAD + ROWS, cols]
                v_edge = jnp.where(row == l, v[l, PAD - 1 : PAD, cols], v_edge)
                if p:
                    u_edge = jnp.where(lane == l, u[l, PAD : PAD + ROWS, lo - 1 : lo], u_edge)
            f_send[m, p, 2 * share] = v_edge
            f_send[m, p, 2 * share + 1] = u_edge
        for c in faces(m):
            c.start()
        f_recv[m, col] = f_send[m, col]

    u0, v0, t0 = ext[0], ext[1], ext[2]
    u1, v1 = advance(u0, v0, t0)
    publish(0, u1, v1)
    t1 = wet * (t0 + 0.1 * lap(t0) + 0.5 * ext[3])
    u2, v2 = advance(u1, v1, t1)
    publish(1, u2, v2)
    saves = [
        pltpu.make_async_copy(a, b, out_sem.at[i])
        for i, (a, b) in enumerate(((u_out, u_dst), (v_out, v_dst), (t_out, t_dst), (h_out, h_dst)))
    ]
    saves += [pltpu.make_async_copy(c_out.at[:, k], c_dst.at[:, k], out_sem.at[4 + k]) for k in range(depth)]
    u_out[...] = u2[:, PAD : PAD + ROWS, :]
    v_out[...] = v2[:, PAD : PAD + ROWS, :]
    saves[0].start()
    saves[1].start()
    t_base[...] = (wet * (t1 + 0.1 * lap(t1)))[:, PAD : PAD + ROWS, :]
    wet_strip[...] = wet[:, PAD : PAD + ROWS, :]

    depth_here = n_in[:, pl.ds(pl.multiple_of(col * LANES, LANES), LANES)]

    def tile_step(m, source, target):
        coefs, sides, light = {}, {}, {}
        state = [jnp.zeros((ROWS, LANES), F32), jnp.ones((ROWS, LANES), F32)]

        def prepare(k):
            if m:
                wait_recv(second(k))
            p, l = k // share, k % share
            u = f_recv[m, p, l]
            v = f_recv[m, p, share + l]
            v_s = jnp.where(row == 0, f_recv[m, p, 2 * share, l : l + 1, :], pltpu.roll(v, 1, 0))
            u_w = jnp.where(lane == 0, f_recv[m, p, 2 * share + 1, :, l : l + 1], pltpu.roll(u, 1, 1))
            a_0 = 1.0 - 0.5 * (
                (jnp.maximum(u, 0.0) - jnp.minimum(u_w, 0.0)) + (jnp.maximum(v, 0.0) - jnp.minimum(v_s, 0.0))
            )
            coefs[k] = (
                a_0, -0.5 * jnp.minimum(u, 0.0), 0.5 * jnp.maximum(u_w, 0.0),
                -0.5 * jnp.minimum(v, 0.0), 0.5 * jnp.maximum(v_s, 0.0),
            )
            sides[k] = jnp.where(
                lane % 2 == 0, pltpu.roll(got_w[m, k], 1, 1), pltpu.roll(got_e[m, k], LANES - 1, 1)
            )

        def advect(k, t):
            a_0, a_e, a_w, a_n, a_s = coefs[k]
            x = source[t, k]
            edge = pltpu.roll(sides[k], (LANES - 2 * t) % LANES, 1)
            x_n = jnp.where(row == ROWS - 1, got_n[m, k, t : t + 1, :], pltpu.roll(x, ROWS - 1, 0))
            x_s = jnp.where(row == 0, got_s[m, k, t : t + 1, :], pltpu.roll(x, 1, 0))
            x_e = jnp.where(lane == LANES - 1, edge, pltpu.roll(x, LANES - 1, 1))
            x_w = jnp.where(lane == 0, edge, pltpu.roll(x, 1, 1))
            return a_0 * x + (a_e * x_e + a_w * x_w) + (a_n * x_n + a_s * x_s)

        def shine(k):
            p, l = k // share, k % share
            prepare(k)
            lead = advect(k, 0)
            wet_k = (k < depth_here).astype(F32)
            tau, top = state
            tau = tau + (0.1 + 0.3 * jnp.maximum(lead, 0.0))
            below = jnp.exp(-tau)
            h_send[m, p, l] = 2.0 * wet_k * (top - below)
            light[k] = (lead, wet_k, top)
            state[:] = [tau, below]
            if k == depth - 1:
                for c in heats(m):
                    c.start()
                h_recv[m, col] = h_send[m, col]

        for k in range(depth):
            if k not in light:
                for ahead in range(k, depth if m and k >= EARLY else k + 1):
                    shine(ahead)
            lead, wet_k, top = light[k]
            adv = jnp.concatenate([lead] + [advect(k, t) for t in range(1, tracers)], axis=0)
            hi = adv.astype(jnp.bfloat16)
            lo = (adv - hi.astype(F32)).astype(jnp.bfloat16)
            both = jnp.dot(rates_hi, jnp.concatenate([hi, lo], axis=1), preferred_element_type=F32)
            r = both[:, :LANES] + both[:, LANES:] + jnp.dot(rates_lo, hi, preferred_element_type=F32)
            new = wet_k * (adv.reshape(tracers, ROWS, LANES) + (0.5 * top) * r.reshape(tracers, ROWS, LANES))
            target[:, k] = new
            if m == 0:
                pack(1, k, new)
                start(second(k))
            else:
                saves[4 + k].start()

    wait_recv(first)
    for c in faces(0):
        c.wait_recv()
    tile_step(0, c_in, c_mid)
    for c in faces(1):
        c.wait_recv()
    tile_step(1, c_mid, c_out)

    for c in heats(0):
        c.wait_recv()
    for p in range(nlon):
        cols = slice(p * LANES, (p + 1) * LANES)
        t_out[:, :, cols] = t_base[:, :, cols] + 0.5 * wet_strip[:, :, cols] * h_recv[0, p]
    saves[2].start()
    wait_send(dyn)
    wait_send(first)
    for k in range(depth):
        wait_send(second(k))
    for m in range(2):
        for c in faces(m):
            c.wait_send()
        for c in heats(m):
            c.wait_send()
    for c in heats(1):
        c.wait_recv()
    for p in range(nlon):
        h_out[:, :, p * LANES : (p + 1) * LANES] = h_recv[1, p]
    saves[3].start()
    for save in saves:
        save.wait()


def store(*refs):
    half = len(refs) // 2
    sems = refs[-1]
    cut = refs[half - 1].shape[0] // CUTS
    pairs = list(zip(refs[: half - 1], refs[half : 2 * half - 1]))
    for i in range(CUTS):
        piece = slice(i * cut, (i + 1) * cut)
        pairs.append((refs[half - 1].at[piece], refs[2 * half - 1].at[piece]))
    copies = [pltpu.make_async_copy(a, b, sems.at[i]) for i, (a, b) in enumerate(pairs)]
    for c in copies:
        c.start()
    for c in copies:
        c.wait()


def shards(sizes, u, v, t, h, c, n, r):
    tracers, depth, share, nlon, _, _ = sizes
    strip = jax.ShapeDtypeStruct(u.shape, F32)
    tile = (ROWS, LANES)
    strip_buf = pltpu.VMEM(u.shape, F32)
    dma = pltpu.SemaphoreType.DMA
    hbm = pl.BlockSpec(memory_space=pltpu.HBM)
    outs = pl.pallas_call(
        functools.partial(kernel, sizes),
        out_shape=(strip, strip, strip, strip, jax.ShapeDtypeStruct(c.shape, F32)),
        in_specs=[hbm] * 7,
        out_specs=(hbm,) * 5,
        scratch_shapes=[
            strip_buf, strip_buf, strip_buf, strip_buf,
            pltpu.VMEM(n.shape, jnp.int32), pltpu.VMEM(n.shape, jnp.int32),
            pltpu.VMEM((4, share, EXT, u.shape[2]), F32),
            pltpu.VMEM((EXT, u.shape[2]), jnp.int32),
            strip_buf, strip_buf,
            pltpu.VMEM(c.shape, F32),
            pltpu.VMEM((2, depth, tracers, LANES), F32),
            pltpu.VMEM((2, depth, tracers, LANES), F32),
            pltpu.VMEM((2, depth) + tile, F32),
            pltpu.VMEM((2, depth, tracers, LANES), F32),
            pltpu.VMEM((2, depth, tracers, LANES), F32),
            pltpu.VMEM((2, depth) + tile, F32),
            pltpu.VMEM((2, depth) + tile, F32),
            pltpu.VMEM((2, nlon, 2 * share + 2) + tile, F32),
            pltpu.VMEM((2, nlon, 2 * share + 2) + tile, F32),
            pltpu.VMEM((2, nlon, share) + tile, F32),
            pltpu.VMEM((2, nlon, share) + tile, F32),
            strip_buf, strip_buf, strip_buf, strip_buf, pltpu.VMEM(c.shape, F32),
            pltpu.VMEM(n.shape, jnp.int32), pltpu.VMEM(r.shape, F32), dma((7,)),
            strip_buf, strip_buf, strip_buf, strip_buf, pltpu.VMEM(c.shape, F32), dma((4 + c.shape[1],)),
            dma((4,)), dma((4,)), dma((4,)), dma((4,)),
            dma((4, depth)), dma((4, depth)),
            dma((2, nlon)), dma((2, nlon)), dma((2, nlon)), dma((2, nlon)),
        ],
        compiler_params=pltpu.CompilerParams(
            collective_id=0, has_side_effects=True, vmem_limit_bytes=VMEM
        ),
    )(u, v, t, h, c, n, r)
    return pl.pallas_call(
        store,
        out_shape=(strip, strip, strip, strip, jax.ShapeDtypeStruct(c.shape, F32)),
        in_specs=[pl.BlockSpec(memory_space=pl.ANY)] * 5,
        out_specs=(hbm,) * 5,
        scratch_shapes=[dma((4 + CUTS,))],
        compiler_params=pltpu.CompilerParams(vmem_limit_bytes=VMEM),
    )(*outs)


def solution(mesh):
    nlon, nrole = mesh.shape["lon"], mesh.shape["role"]
    nstrip = mesh.shape["lat"] * nrole
    strip = P("lon", ("grp", "lat", "role"), None)
    tile = P(None, None, ("grp", "lat", "role"), "lon")

    def run(u, v, t, h, c, n, r):
        sizes = (c.shape[0], c.shape[1], u.shape[0] // nlon, nlon, nrole, nstrip)
        return jax.shard_map(
            functools.partial(shards, sizes),
            mesh=mesh,
            in_specs=(strip, strip, strip, strip, tile, P(("grp", "lat", "role"), None), P()),
            out_specs=(strip, strip, strip, strip, tile),
            check_vma=False,
        )(u, v, t, h, c, n, r)

    return run
```

```python
import functools

import jax
import jax.numpy as jnp
from jax import lax
from jax.experimental import pallas as pl
from jax.experimental.pallas import tpu as pltpu
from jax.sharding import PartitionSpec as P

ROWS = 8
LANES = 128
PAD = 4
EXT = ROWS + 2 * PAD
EARLY = 5
VMEM = 64 * 1024 * 1024
CUTS = 4
F32 = jnp.float32


def east(q):
    lane = lax.broadcasted_iota(jnp.int32, q.shape, q.ndim - 1)
    return jnp.where(lane < q.shape[-1] - 1, pltpu.roll(q, q.shape[-1] - 1, q.ndim - 1), 0.0)


def west(q):
    lane = lax.broadcasted_iota(jnp.int32, q.shape, q.ndim - 1)
    return jnp.where(lane > 0, pltpu.roll(q, 1, q.ndim - 1), 0.0)


def north(q):
    return pltpu.roll(q, q.shape[-2] - 1, q.ndim - 2)


def south(q):
    return pltpu.roll(q, 1, q.ndim - 2)


def lap(q):
    return east(q) + west(q) + north(q) + south(q) - 4.0 * q


def kernel(
    sizes,
    u_hbm, v_hbm, t_hbm, h_hbm, c_hbm, n_hbm, r_hbm,
    u_dst, v_dst, t_dst, h_dst, c_dst,
    pk_n, pk_s, rc_n, rc_s, cnt_n, cnt_s, ext, ext_n, t_base, wet_strip,
    c_mid, row_lo, row_hi, col_ed, got_n, got_s, got_w, got_e,
    f_send, f_recv, h_send, h_recv,
    u_in, v_in, t_in, h_in, c_in, n_in, r_in, in_sem,
    u_out, v_out, t_out, h_out, c_out, out_sem,
    d_ssem, d_rsem, c0_ssem, c0_rsem, c1_ssem, c1_rsem, f_ssem, f_rsem, h_ssem, h_rsem,
):
    tracers, depth, share, nlon, nrole, nstrip = sizes
    width = nlon * LANES
    arrays = (
        (u_hbm, u_in), (v_hbm, v_in), (t_hbm, t_in), (h_hbm, h_in), (n_hbm, n_in), (c_hbm, c_in), (r_hbm, r_in),
    )
    loads = [pltpu.make_async_copy(a, b, in_sem.at[i]) for i, (a, b) in enumerate(arrays)]
    for load in loads:
        load.start()
    s = lax.axis_index("lat") * nrole + lax.axis_index("role")
    col = lax.axis_index("lon")
    has_n, has_s = s < nstrip - 1, s > 0
    has_e, has_w = col < nlon - 1, col > 0
    sn, ss = lax.rem(s + 1, nstrip), lax.rem(s + nstrip - 1, nstrip)
    dev_n = {"lat": sn // nrole, "role": lax.rem(sn, nrole)}
    dev_s = {"lat": ss // nrole, "role": lax.rem(ss, nrole)}
    dev_e = {"lon": lax.rem(col + 1, nlon)}
    dev_w = {"lon": lax.rem(col + nlon - 1, nlon)}

    barrier = pltpu.get_barrier_semaphore()

    def greet(dev):
        pl.semaphore_signal(barrier, inc=1, device_id=dev, device_id_type=pl.DeviceIdType.MESH)

    pl.when(has_n)(lambda: greet(dev_n))
    pl.when(has_s)(lambda: greet(dev_s))
    for d in range(1, nlon):
        greet({"lon": lax.rem(col + d, nlon)})

    def copy(src, dst, ssem, rsem, dev):
        return pltpu.make_async_remote_copy(
            src_ref=src, dst_ref=dst, send_sem=ssem, recv_sem=rsem,
            device_id=dev, device_id_type=pl.DeviceIdType.MESH,
        )

    def start(copies):
        for c, send, _ in copies:
            pl.when(send)(c.start)

    def wait_recv(copies):
        for c, _, recv in copies:
            pl.when(recv)(c.wait_recv)

    def wait_send(copies):
        for c, send, _ in copies:
            pl.when(send)(c.wait_send)

    for load in loads[:5]:
        load.wait()
    pk_n[:, 0:3, :] = v_in[:, 5:8, :]
    pk_n[:, 3:5, :] = u_in[:, 6:8, :]
    pk_n[:, 5:7, :] = t_in[:, 6:8, :]
    pk_n[:, 7:8, :] = h_in[:, 7:8, :]
    pk_s[:, 0:2, :] = u_in[:, 0:2, :]
    pk_s[:, 2:4, :] = v_in[:, 0:2, :]
    pk_s[:, 4:6, :] = t_in[:, 0:2, :]
    pk_s[:, 6:7, :] = h_in[:, 0:1, :]
    pk_s[:, 7:8, :] = h_in[:, 0:1, :]

    lane = lax.broadcasted_iota(jnp.int32, (ROWS, LANES), 1)
    row = lax.broadcasted_iota(jnp.int32, (ROWS, LANES), 0)

    def pack(m, k, x):
        row_lo[m, k] = x[:, 0, :]
        row_hi[m, k] = x[:, ROWS - 1, :]
        acc = x[0]
        for t in range(1, tracers):
            here = (lane == 2 * t - 1) | (lane == 2 * t)
            acc = jnp.where(here, pltpu.roll(x[t], 2 * t, 1), acc)
        col_ed[m, k] = acc

    dyn = [
        (copy(pk_n, rc_s, d_ssem.at[0], d_rsem.at[0], dev_n), has_n, has_s),
        (copy(pk_s, rc_n, d_ssem.at[1], d_rsem.at[1], dev_s), has_s, has_n),
        (copy(n_in, cnt_s, d_ssem.at[2], d_rsem.at[2], dev_n), has_n, has_s),
        (copy(n_in, cnt_n, d_ssem.at[3], d_rsem.at[3], dev_s), has_s, has_n),
    ]
    first = [
        (copy(row_hi.at[0], got_s.at[0], c0_ssem.at[0], c0_rsem.at[0], dev_n), has_n, has_s),
        (copy(row_lo.at[0], got_n.at[0], c0_ssem.at[1], c0_rsem.at[1], dev_s), has_s, has_n),
        (copy(col_ed.at[0], got_w.at[0], c0_ssem.at[2], c0_rsem.at[2], dev_e), has_e, has_w),
        (copy(col_ed.at[0], got_e.at[0], c0_ssem.at[3], c0_rsem.at[3], dev_w), has_w, has_e),
    ]

    def second(k):
        return [
            (copy(row_hi.at[1, k], got_s.at[1, k], c1_ssem.at[0, k], c1_rsem.at[0, k], dev_n), has_n, has_s),
            (copy(row_lo.at[1, k], got_n.at[1, k], c1_ssem.at[1, k], c1_rsem.at[1, k], dev_s), has_s, has_n),
            (copy(col_ed.at[1, k], got_w.at[1, k], c1_ssem.at[2, k], c1_rsem.at[2, k], dev_e), has_e, has_w),
            (copy(col_ed.at[1, k], got_e.at[1, k], c1_ssem.at[3, k], c1_rsem.at[3, k], dev_w), has_w, has_e),
        ]

    def faces(m):
        out = []
        for d in range(1, nlon):
            p = lax.rem(col + d, nlon)
            out.append(copy(f_send.at[m, p], f_recv.at[m, col], f_ssem.at[m, d], f_rsem.at[m, d], {"lon": p}))
        return out

    def heats(m):
        out = []
        for d in range(1, nlon):
            p = lax.rem(col + d, nlon)
            out.append(copy(h_send.at[m, p], h_recv.at[m, col], h_ssem.at[m, d], h_rsem.at[m, d], {"lon": p}))
        return out

    pl.semaphore_wait(barrier, nlon - 1 + jnp.minimum(s, 1) + jnp.minimum(nstrip - 1 - s, 1))
    start(dyn)
    for load in loads[5:]:
        load.wait()
    for k in range(depth):
        pack(0, k, c_in[:, k])
    start(first)

    @pl.when(jnp.logical_not(has_s))
    def _():
        rc_s[...] = jnp.zeros_like(rc_s)
        cnt_s[...] = jnp.zeros_like(cnt_s)
        got_s[...] = jnp.zeros_like(got_s)

    @pl.when(jnp.logical_not(has_n))
    def _():
        rc_n[...] = jnp.zeros_like(rc_n)
        cnt_n[...] = jnp.zeros_like(cnt_n)
        got_n[...] = jnp.zeros_like(got_n)

    @pl.when(jnp.logical_not(has_w))
    def _():
        got_w[...] = jnp.zeros_like(got_w)

    @pl.when(jnp.logical_not(has_e))
    def _():
        got_e[...] = jnp.zeros_like(got_e)

    wide = tracers * ROWS
    spread = (
        lax.broadcasted_iota(jnp.int32, (wide, tracers), 0) // ROWS
        == lax.broadcasted_iota(jnp.int32, (wide, tracers), 1)
    ).astype(F32)
    gather = (
        lax.broadcasted_iota(jnp.int32, (tracers, wide), 1) // ROWS
        == lax.broadcasted_iota(jnp.int32, (tracers, wide), 0)
    ).astype(F32)
    exact = lax.Precision.HIGHEST
    rates = jnp.dot(
        spread, jnp.dot(r_in[...], gather, precision=exact, preferred_element_type=F32),
        precision=exact, preferred_element_type=F32,
    )
    same_row = (
        lax.broadcasted_iota(jnp.int32, (wide, wide), 0) % ROWS
        == lax.broadcasted_iota(jnp.int32, (wide, wide), 1) % ROWS
    )
    rates = jnp.where(same_row, rates, 0.0)
    rates_hi = rates.astype(jnp.bfloat16)
    rates_lo = (rates - rates_hi.astype(F32)).astype(jnp.bfloat16)

    zero = jnp.zeros((share, PAD, width), F32)
    for f in range(4):
        ext[f, :, 0:PAD, :] = zero
        ext[f, :, PAD + ROWS :, :] = zero
    ext_n[0:PAD, :] = jnp.zeros((PAD, width), jnp.int32)
    ext_n[PAD + ROWS :, :] = jnp.zeros((PAD, width), jnp.int32)
    for f, ref in enumerate((u_in, v_in, t_in, h_in)):
        ext[f, :, PAD : PAD + ROWS, :] = ref[...]
    ext_n[PAD : PAD + ROWS, :] = n_in[...]

    wait_recv(dyn)
    ext[0, :, 2:4, :] = rc_s[:, 3:5, :]
    ext[1, :, 1:4, :] = rc_s[:, 0:3, :]
    ext[2, :, 2:4, :] = rc_s[:, 5:7, :]
    ext[3, :, 3:4, :] = rc_s[:, 7:8, :]
    ext[0, :, 12:14, :] = rc_n[:, 0:2, :]
    ext[1, :, 12:14, :] = rc_n[:, 2:4, :]
    ext[2, :, 12:14, :] = rc_n[:, 4:6, :]
    ext[3, :, 12:13, :] = rc_n[:, 6:7, :]
    ext_n[2:4, :] = cnt_s[6:8, :]
    ext_n[12:14, :] = cnt_n[0:2, :]

    shape = (share, EXT, width)
    level = col * share + lax.broadcasted_iota(jnp.int32, shape, 0)
    wet = (level < ext_n[...][None]).astype(F32)
    wet_u = wet * east(wet)
    wet_v = wet * north(wet)
    spot = (s * ROWS - PAD + lax.broadcasted_iota(jnp.int32, shape, 1)).astype(F32)
    fcor = 0.3 * (2.0 * (spot + 0.5) / (nstrip * ROWS) - 1.0)

    def advance(u, v, t):
        new_u = wet_u * (u + 0.1 * lap(u) + fcor * v - 0.2 * (east(t) - t))
        new_v = wet_v * (v + 0.1 * lap(v) - fcor * u - 0.2 * (north(t) - t))
        return new_u, new_v

    def publish(m, u, v):
        for p in range(nlon):
            lo = p * LANES
            cols = slice(lo, lo + LANES)
            v_edge = jnp.zeros((ROWS, LANES), F32)
            u_edge = jnp.zeros((ROWS, LANES), F32)
            for l in range(share):
                f_send[m, p, l] = u[l, PAD : PAD + ROWS, cols]
                f_send[m, p, share + l] = v[l, PAD : PAD + ROWS, cols]
                v_edge = jnp.where(row == l, v[l, PAD - 1 : PAD, cols], v_edge)
                if p:
                    u_edge = jnp.where(lane == l, u[l, PAD : PAD + ROWS, lo - 1 : lo], u_edge)
            f_send[m, p, 2 * share] = v_edge
            f_send[m, p, 2 * share + 1] = u_edge
        for c in faces(m):
            c.start()
        f_recv[m, col] = f_send[m, col]

    u0, v0, t0 = ext[0], ext[1], ext[2]
    u1, v1 = advance(u0, v0, t0)
    publish(0, u1, v1)
    t1 = wet * (t0 + 0.1 * lap(t0) + 0.5 * ext[3])
    u2, v2 = advance(u1, v1, t1)
    publish(1, u2, v2)
    saves = [
        pltpu.make_async_copy(a, b, out_sem.at[i])
        for i, (a, b) in enumerate(((u_out, u_dst), (v_out, v_dst), (t_out, t_dst), (h_out, h_dst)))
    ]
    saves += [pltpu.make_async_copy(c_out.at[:, k], c_dst.at[:, k], out_sem.at[4 + k]) for k in range(depth)]
    u_out[...] = u2[:, PAD : PAD + ROWS, :]
    v_out[...] = v2[:, PAD : PAD + ROWS, :]
    saves[0].start()
    saves[1].start()
    t_base[...] = (wet * (t1 + 0.1 * lap(t1)))[:, PAD : PAD + ROWS, :]
    wet_strip[...] = wet[:, PAD : PAD + ROWS, :]

    depth_here = n_in[:, pl.ds(pl.multiple_of(col * LANES, LANES), LANES)]

    def tile_step(m, source, target):
        coefs, sides, light = {}, {}, {}
        state = [jnp.zeros((ROWS, LANES), F32), jnp.ones((ROWS, LANES), F32)]

        def prepare(k):
            if m:
                wait_recv(second(k))
            p, l = k // share, k % share
            u = f_recv[m, p, l]
            v = f_recv[m, p, share + l]
            v_s = jnp.where(row == 0, f_recv[m, p, 2 * share, l : l + 1, :], pltpu.roll(v, 1, 0))
            u_w = jnp.where(lane == 0, f_recv[m, p, 2 * share + 1, :, l : l + 1], pltpu.roll(u, 1, 1))
            a_0 = 1.0 - 0.5 * (
                (jnp.maximum(u, 0.0) - jnp.minimum(u_w, 0.0)) + (jnp.maximum(v, 0.0) - jnp.minimum(v_s, 0.0))
            )
            coefs[k] = (
                a_0, -0.5 * jnp.minimum(u, 0.0), 0.5 * jnp.maximum(u_w, 0.0),
                -0.5 * jnp.minimum(v, 0.0), 0.5 * jnp.maximum(v_s, 0.0),
            )
            sides[k] = jnp.where(
                lane % 2 == 0, pltpu.roll(got_w[m, k], 1, 1), pltpu.roll(got_e[m, k], LANES - 1, 1)
            )

        def advect(k, t):
            a_0, a_e, a_w, a_n, a_s = coefs[k]
            x = source[t, k]
            edge = pltpu.roll(sides[k], (LANES - 2 * t) % LANES, 1)
            x_n = jnp.where(row == ROWS - 1, got_n[m, k, t : t + 1, :], pltpu.roll(x, ROWS - 1, 0))
            x_s = jnp.where(row == 0, got_s[m, k, t : t + 1, :], pltpu.roll(x, 1, 0))
            x_e = jnp.where(lane == LANES - 1, edge, pltpu.roll(x, LANES - 1, 1))
            x_w = jnp.where(lane == 0, edge, pltpu.roll(x, 1, 1))
            return a_0 * x + (a_e * x_e + a_w * x_w) + (a_n * x_n + a_s * x_s)

        def shine(k):
            p, l = k // share, k % share
            prepare(k)
            lead = advect(k, 0)
            wet_k = (k < depth_here).astype(F32)
            tau, top = state
            tau = tau + (0.1 + 0.3 * jnp.maximum(lead, 0.0))
            below = jnp.exp(-tau)
            h_send[m, p, l] = 2.0 * wet_k * (top - below)
            light[k] = (lead, wet_k, top)
            state[:] = [tau, below]
            if k == depth - 1:
                for c in heats(m):
                    c.start()
                h_recv[m, col] = h_send[m, col]

        for k in range(depth):
            if k not in light:
                for ahead in range(k, depth if m and k >= EARLY else k + 1):
                    shine(ahead)
            lead, wet_k, top = light[k]
            adv = jnp.concatenate([lead] + [advect(k, t) for t in range(1, tracers)], axis=0)
            hi = adv.astype(jnp.bfloat16)
            lo = (adv - hi.astype(F32)).astype(jnp.bfloat16)
            both = jnp.dot(rates_hi, jnp.concatenate([hi, lo], axis=1), preferred_element_type=F32)
            r = both[:, :LANES] + both[:, LANES:] + jnp.dot(rates_lo, hi, preferred_element_type=F32)
            new = wet_k * (adv.reshape(tracers, ROWS, LANES) + (0.5 * top) * r.reshape(tracers, ROWS, LANES))
            target[:, k] = new
            if m == 0:
                pack(1, k, new)
                start(second(k))
            else:
                saves[4 + k].start()

    wait_recv(first)
    for c in faces(0):
        c.wait_recv()
    tile_step(0, c_in, c_mid)
    for c in faces(1):
        c.wait_recv()
    tile_step(1, c_mid, c_out)

    for c in heats(0):
        c.wait_recv()
    for p in range(nlon):
        cols = slice(p * LANES, (p + 1) * LANES)
        t_out[:, :, cols] = t_base[:, :, cols] + 0.5 * wet_strip[:, :, cols] * h_recv[0, p]
    saves[2].start()
    wait_send(dyn)
    wait_send(first)
    for k in range(depth):
        wait_send(second(k))
    for m in range(2):
        for c in faces(m):
            c.wait_send()
        for c in heats(m):
            c.wait_send()
    for c in heats(1):
        c.wait_recv()
    for p in range(nlon):
        h_out[:, :, p * LANES : (p + 1) * LANES] = h_recv[1, p]
    saves[3].start()
    for save in saves:
        save.wait()


def store(*refs):
    half = len(refs) // 3
    sources, results, held, (load_sem, save_sem) = refs[:half], refs[half : 2 * half], refs[2 * half : -2], refs[-2:]
    cut = sources[-1].shape[0] // CUTS
    pieces = [(i, slice(None)) for i in range(half - 1)]
    pieces = [(half - 1, slice(i * cut, (i + 1) * cut)) for i in range(CUTS)] + pieces
    loads, saves = [], []
    for n, (i, piece) in enumerate(pieces):
        loads.append(pltpu.make_async_copy(sources[i].at[piece], held[i].at[piece], load_sem.at[n]))
        saves.append(pltpu.make_async_copy(held[i].at[piece], results[i].at[piece], save_sem.at[n]))
    for load in loads:
        load.start()
    for load, save in zip(loads, saves):
        load.wait()
        save.start()
    for save in saves:
        save.wait()


def shards(sizes, u, v, t, h, c, n, r):
    tracers, depth, share, nlon, _, _ = sizes
    strip = jax.ShapeDtypeStruct(u.shape, F32)
    tile = (ROWS, LANES)
    strip_buf = pltpu.VMEM(u.shape, F32)
    dma = pltpu.SemaphoreType.DMA
    hbm = pl.BlockSpec(memory_space=pltpu.HBM)
    outs = pl.pallas_call(
        functools.partial(kernel, sizes),
        out_shape=(strip, strip, strip, strip, jax.ShapeDtypeStruct(c.shape, F32)),
        in_specs=[hbm] * 7,
        out_specs=(hbm,) * 5,
        scratch_shapes=[
            strip_buf, strip_buf, strip_buf, strip_buf,
            pltpu.VMEM(n.shape, jnp.int32), pltpu.VMEM(n.shape, jnp.int32),
            pltpu.VMEM((4, share, EXT, u.shape[2]), F32),
            pltpu.VMEM((EXT, u.shape[2]), jnp.int32),
            strip_buf, strip_buf,
            pltpu.VMEM(c.shape, F32),
            pltpu.VMEM((2, depth, tracers, LANES), F32),
            pltpu.VMEM((2, depth, tracers, LANES), F32),
            pltpu.VMEM((2, depth) + tile, F32),
            pltpu.VMEM((2, depth, tracers, LANES), F32),
            pltpu.VMEM((2, depth, tracers, LANES), F32),
            pltpu.VMEM((2, depth) + tile, F32),
            pltpu.VMEM((2, depth) + tile, F32),
            pltpu.VMEM((2, nlon, 2 * share + 2) + tile, F32),
            pltpu.VMEM((2, nlon, 2 * share + 2) + tile, F32),
            pltpu.VMEM((2, nlon, share) + tile, F32),
            pltpu.VMEM((2, nlon, share) + tile, F32),
            strip_buf, strip_buf, strip_buf, strip_buf, pltpu.VMEM(c.shape, F32),
            pltpu.VMEM(n.shape, jnp.int32), pltpu.VMEM(r.shape, F32), dma((7,)),
            strip_buf, strip_buf, strip_buf, strip_buf, pltpu.VMEM(c.shape, F32), dma((4 + c.shape[1],)),
            dma((4,)), dma((4,)), dma((4,)), dma((4,)),
            dma((4, depth)), dma((4, depth)),
            dma((2, nlon)), dma((2, nlon)), dma((2, nlon)), dma((2, nlon)),
        ],
        compiler_params=pltpu.CompilerParams(
            collective_id=0, has_side_effects=True, vmem_limit_bytes=VMEM
        ),
    )(u, v, t, h, c, n, r)
    return pl.pallas_call(
        store,
        out_shape=(strip, strip, strip, strip, jax.ShapeDtypeStruct(c.shape, F32)),
        in_specs=[hbm] * 5,
        out_specs=(hbm,) * 5,
        scratch_shapes=[strip_buf] * 4 + [pltpu.VMEM(c.shape, F32), dma((4 + CUTS,)), dma((4 + CUTS,))],
        compiler_params=pltpu.CompilerParams(vmem_limit_bytes=VMEM),
    )(*outs)


def solution(mesh):
    nlon, nrole = mesh.shape["lon"], mesh.shape["role"]
    nstrip = mesh.shape["lat"] * nrole
    strip = P("lon", ("grp", "lat", "role"), None)
    tile = P(None, None, ("grp", "lat", "role"), "lon")

    def run(u, v, t, h, c, n, r):
        sizes = (c.shape[0], c.shape[1], u.shape[0] // nlon, nlon, nrole, nstrip)
        return jax.shard_map(
            functools.partial(shards, sizes),
            mesh=mesh,
            in_specs=(strip, strip, strip, strip, tile, P(("grp", "lat", "role"), None), P()),
            out_specs=(strip, strip, strip, strip, tile),
            check_vma=False,
        )(u, v, t, h, c, n, r)

    return run
```

```python
import functools

import jax
import jax.numpy as jnp
from jax import lax
from jax.experimental import pallas as pl
from jax.experimental.pallas import tpu as pltpu
from jax.sharding import PartitionSpec as P

ROWS = 8
LANES = 128
PAD = 4
EXT = ROWS + 2 * PAD
PAIR = 2
VMEM = 64 * 1024 * 1024
CUTS = 8
F32 = jnp.float32


def east(q):
    lane = lax.broadcasted_iota(jnp.int32, q.shape, q.ndim - 1)
    return jnp.where(lane < q.shape[-1] - 1, pltpu.roll(q, q.shape[-1] - 1, q.ndim - 1), 0.0)


def west(q):
    lane = lax.broadcasted_iota(jnp.int32, q.shape, q.ndim - 1)
    return jnp.where(lane > 0, pltpu.roll(q, 1, q.ndim - 1), 0.0)


def north(q):
    return pltpu.roll(q, q.shape[-2] - 1, q.ndim - 2)


def south(q):
    return pltpu.roll(q, 1, q.ndim - 2)


def lap(q):
    return east(q) + west(q) + north(q) + south(q) - 4.0 * q


def kernel(
    sizes,
    u_hbm, v_hbm, t_hbm, h_hbm, c_hbm, n_hbm, r_hbm,
    u_dst, v_dst, t_dst, h_dst, c_dst,
    pk_n, pk_s, rc_n, rc_s, cnt_n, cnt_s, ext, ext_n, t_base, wet_strip,
    c_mid, row_lo, row_hi, col_ed, got_n, got_s, got_w, got_e,
    f_send, f_recv, h_send, h_recv,
    u_in, v_in, t_in, h_in, c_in, n_in, r_in, in_sem,
    u_out, v_out, t_out, h_out, c_out, out_sem,
    d_ssem, d_rsem, c0_ssem, c0_rsem, c1_ssem, c1_rsem, f_ssem, f_rsem, h_ssem, h_rsem,
):
    tracers, depth, share, nlon, nrole, nstrip = sizes
    width = nlon * LANES
    arrays = (
        (u_hbm, u_in), (v_hbm, v_in), (t_hbm, t_in), (h_hbm, h_in), (n_hbm, n_in), (c_hbm, c_in), (r_hbm, r_in),
    )
    loads = [pltpu.make_async_copy(a, b, in_sem.at[i]) for i, (a, b) in enumerate(arrays)]
    for load in loads:
        load.start()
    s = lax.axis_index("lat") * nrole + lax.axis_index("role")
    col = lax.axis_index("lon")
    has_n, has_s = s < nstrip - 1, s > 0
    has_e, has_w = col < nlon - 1, col > 0
    sn, ss = lax.rem(s + 1, nstrip), lax.rem(s + nstrip - 1, nstrip)
    dev_n = {"lat": sn // nrole, "role": lax.rem(sn, nrole)}
    dev_s = {"lat": ss // nrole, "role": lax.rem(ss, nrole)}
    dev_e = {"lon": lax.rem(col + 1, nlon)}
    dev_w = {"lon": lax.rem(col + nlon - 1, nlon)}

    barrier = pltpu.get_barrier_semaphore()

    def greet(dev):
        pl.semaphore_signal(barrier, inc=1, device_id=dev, device_id_type=pl.DeviceIdType.MESH)

    pl.when(has_n)(lambda: greet(dev_n))
    pl.when(has_s)(lambda: greet(dev_s))
    for d in range(1, nlon):
        greet({"lon": lax.rem(col + d, nlon)})

    def copy(src, dst, ssem, rsem, dev):
        return pltpu.make_async_remote_copy(
            src_ref=src, dst_ref=dst, send_sem=ssem, recv_sem=rsem,
            device_id=dev, device_id_type=pl.DeviceIdType.MESH,
        )

    def start(copies):
        for c, send, _ in copies:
            pl.when(send)(c.start)

    def wait_recv(copies):
        for c, _, recv in copies:
            pl.when(recv)(c.wait_recv)

    def wait_send(copies):
        for c, send, _ in copies:
            pl.when(send)(c.wait_send)

    for load in loads[:5]:
        load.wait()
    pk_n[:, 0:3, :] = v_in[:, 5:8, :]
    pk_n[:, 3:5, :] = u_in[:, 6:8, :]
    pk_n[:, 5:7, :] = t_in[:, 6:8, :]
    pk_n[:, 7:8, :] = h_in[:, 7:8, :]
    pk_s[:, 0:2, :] = u_in[:, 0:2, :]
    pk_s[:, 2:4, :] = v_in[:, 0:2, :]
    pk_s[:, 4:6, :] = t_in[:, 0:2, :]
    pk_s[:, 6:7, :] = h_in[:, 0:1, :]
    pk_s[:, 7:8, :] = h_in[:, 0:1, :]

    lane = lax.broadcasted_iota(jnp.int32, (ROWS, LANES), 1)
    row = lax.broadcasted_iota(jnp.int32, (ROWS, LANES), 0)

    def pack(m, k, x):
        row_lo[m, k] = x[:, 0, :]
        row_hi[m, k] = x[:, ROWS - 1, :]
        acc = x[0]
        for t in range(1, tracers):
            here = (lane == 2 * t - 1) | (lane == 2 * t)
            acc = jnp.where(here, pltpu.roll(x[t], 2 * t, 1), acc)
        col_ed[m, k] = acc

    dyn = [
        (copy(pk_n, rc_s, d_ssem.at[0], d_rsem.at[0], dev_n), has_n, has_s),
        (copy(pk_s, rc_n, d_ssem.at[1], d_rsem.at[1], dev_s), has_s, has_n),
        (copy(n_in, cnt_s, d_ssem.at[2], d_rsem.at[2], dev_n), has_n, has_s),
        (copy(n_in, cnt_n, d_ssem.at[3], d_rsem.at[3], dev_s), has_s, has_n),
    ]
    first = [
        (copy(row_hi.at[0], got_s.at[0], c0_ssem.at[0], c0_rsem.at[0], dev_n), has_n, has_s),
        (copy(row_lo.at[0], got_n.at[0], c0_ssem.at[1], c0_rsem.at[1], dev_s), has_s, has_n),
        (copy(col_ed.at[0], got_w.at[0], c0_ssem.at[2], c0_rsem.at[2], dev_e), has_e, has_w),
        (copy(col_ed.at[0], got_e.at[0], c0_ssem.at[3], c0_rsem.at[3], dev_w), has_w, has_e),
    ]

    def second(g):
        two = pl.ds(g * PAIR, PAIR)
        routes = (
            (row_hi, got_s, dev_n, has_n, has_s), (row_lo, got_n, dev_s, has_s, has_n),
            (col_ed, got_w, dev_e, has_e, has_w), (col_ed, got_e, dev_w, has_w, has_e),
        )
        return [
            (copy(a.at[1, two], b.at[1, two], c1_ssem.at[i, g], c1_rsem.at[i, g], dev), send, recv)
            for i, (a, b, dev, send, recv) in enumerate(routes)
        ]

    def faces(m):
        out = []
        for d in range(1, nlon):
            p = lax.rem(col + d, nlon)
            out.append(copy(f_send.at[m, p], f_recv.at[m, col], f_ssem.at[m, d], f_rsem.at[m, d], {"lon": p}))
        return out

    def heats(m):
        out = []
        for d in range(1, nlon):
            p = lax.rem(col + d, nlon)
            out.append(copy(h_send.at[m, p], h_recv.at[m, col], h_ssem.at[m, d], h_rsem.at[m, d], {"lon": p}))
        return out

    pl.semaphore_wait(barrier, nlon - 1 + jnp.minimum(s, 1) + jnp.minimum(nstrip - 1 - s, 1))
    start(dyn)
    for load in loads[5:]:
        load.wait()
    for k in range(depth):
        pack(0, k, c_in[:, k])
    start(first)

    @pl.when(jnp.logical_not(has_s))
    def _():
        rc_s[...] = jnp.zeros_like(rc_s)
        cnt_s[...] = jnp.zeros_like(cnt_s)
        got_s[...] = jnp.zeros_like(got_s)

    @pl.when(jnp.logical_not(has_n))
    def _():
        rc_n[...] = jnp.zeros_like(rc_n)
        cnt_n[...] = jnp.zeros_like(cnt_n)
        got_n[...] = jnp.zeros_like(got_n)

    @pl.when(jnp.logical_not(has_w))
    def _():
        got_w[...] = jnp.zeros_like(got_w)

    @pl.when(jnp.logical_not(has_e))
    def _():
        got_e[...] = jnp.zeros_like(got_e)

    wide = tracers * ROWS
    spread = (
        lax.broadcasted_iota(jnp.int32, (wide, tracers), 0) // ROWS
        == lax.broadcasted_iota(jnp.int32, (wide, tracers), 1)
    ).astype(F32)
    gather = (
        lax.broadcasted_iota(jnp.int32, (tracers, wide), 1) // ROWS
        == lax.broadcasted_iota(jnp.int32, (tracers, wide), 0)
    ).astype(F32)
    exact = lax.Precision.HIGHEST
    rates = jnp.dot(
        spread, jnp.dot(r_in[...], gather, precision=exact, preferred_element_type=F32),
        precision=exact, preferred_element_type=F32,
    )
    same_row = (
        lax.broadcasted_iota(jnp.int32, (wide, wide), 0) % ROWS
        == lax.broadcasted_iota(jnp.int32, (wide, wide), 1) % ROWS
    )
    rates = jnp.where(same_row, rates, 0.0)
    rates_hi = rates.astype(jnp.bfloat16)
    rates_lo = (rates - rates_hi.astype(F32)).astype(jnp.bfloat16)

    zero = jnp.zeros((share, PAD, width), F32)
    for f in range(4):
        ext[f, :, 0:PAD, :] = zero
        ext[f, :, PAD + ROWS :, :] = zero
    ext_n[0:PAD, :] = jnp.zeros((PAD, width), jnp.int32)
    ext_n[PAD + ROWS :, :] = jnp.zeros((PAD, width), jnp.int32)
    for f, ref in enumerate((u_in, v_in, t_in, h_in)):
        ext[f, :, PAD : PAD + ROWS, :] = ref[...]
    ext_n[PAD : PAD + ROWS, :] = n_in[...]

    wait_recv(dyn)
    ext[0, :, 2:4, :] = rc_s[:, 3:5, :]
    ext[1, :, 1:4, :] = rc_s[:, 0:3, :]
    ext[2, :, 2:4, :] = rc_s[:, 5:7, :]
    ext[3, :, 3:4, :] = rc_s[:, 7:8, :]
    ext[0, :, 12:14, :] = rc_n[:, 0:2, :]
    ext[1, :, 12:14, :] = rc_n[:, 2:4, :]
    ext[2, :, 12:14, :] = rc_n[:, 4:6, :]
    ext[3, :, 12:13, :] = rc_n[:, 6:7, :]
    ext_n[2:4, :] = cnt_s[6:8, :]
    ext_n[12:14, :] = cnt_n[0:2, :]

    shape = (share, EXT, width)
    level = col * share + lax.broadcasted_iota(jnp.int32, shape, 0)
    wet = (level < ext_n[...][None]).astype(F32)
    wet_u = wet * east(wet)
    wet_v = wet * north(wet)
    spot = (s * ROWS - PAD + lax.broadcasted_iota(jnp.int32, shape, 1)).astype(F32)
    fcor = 0.3 * (2.0 * (spot + 0.5) / (nstrip * ROWS) - 1.0)

    def advance(u, v, t):
        new_u = wet_u * (u + 0.1 * lap(u) + fcor * v - 0.2 * (east(t) - t))
        new_v = wet_v * (v + 0.1 * lap(v) - fcor * u - 0.2 * (north(t) - t))
        return new_u, new_v

    def publish(m, u, v):
        for p in range(nlon):
            lo = p * LANES
            cols = slice(lo, lo + LANES)
            v_edge = jnp.zeros((ROWS, LANES), F32)
            u_edge = jnp.zeros((ROWS, LANES), F32)
            for l in range(share):
                f_send[m, p, l] = u[l, PAD : PAD + ROWS, cols]
                f_send[m, p, share + l] = v[l, PAD : PAD + ROWS, cols]
                v_edge = jnp.where(row == l, v[l, PAD - 1 : PAD, cols], v_edge)
                if p:
                    u_edge = jnp.where(lane == l, u[l, PAD : PAD + ROWS, lo - 1 : lo], u_edge)
            f_send[m, p, 2 * share] = v_edge
            f_send[m, p, 2 * share + 1] = u_edge
        for c in faces(m):
            c.start()
        f_recv[m, col] = f_send[m, col]

    u0, v0, t0 = ext[0], ext[1], ext[2]
    u1, v1 = advance(u0, v0, t0)
    publish(0, u1, v1)
    t1 = wet * (t0 + 0.1 * lap(t0) + 0.5 * ext[3])
    u2, v2 = advance(u1, v1, t1)
    publish(1, u2, v2)
    saves = [
        pltpu.make_async_copy(a, b, out_sem.at[i])
        for i, (a, b) in enumerate(((u_out, u_dst), (v_out, v_dst), (t_out, t_dst), (h_out, h_dst)))
    ]
    saves += [pltpu.make_async_copy(c_out.at[:, k], c_dst.at[:, k], out_sem.at[4 + k]) for k in range(depth)]
    u_out[...] = u2[:, PAD : PAD + ROWS, :]
    v_out[...] = v2[:, PAD : PAD + ROWS, :]
    saves[0].start()
    saves[1].start()
    t_base[...] = (wet * (t1 + 0.1 * lap(t1)))[:, PAD : PAD + ROWS, :]
    wet_strip[...] = wet[:, PAD : PAD + ROWS, :]

    depth_here = n_in[:, pl.ds(pl.multiple_of(col * LANES, LANES), LANES)]

    def tile_step(m, source, target):
        coefs, sides, light = {}, {}, {}
        state = [jnp.zeros((ROWS, LANES), F32), jnp.ones((ROWS, LANES), F32)]

        def prepare(k):
            p, l = k // share, k % share
            u = f_recv[m, p, l]
            v = f_recv[m, p, share + l]
            v_s = jnp.where(row == 0, f_recv[m, p, 2 * share, l : l + 1, :], pltpu.roll(v, 1, 0))
            u_w = jnp.where(lane == 0, f_recv[m, p, 2 * share + 1, :, l : l + 1], pltpu.roll(u, 1, 1))
            a_0 = 1.0 - 0.5 * (
                (jnp.maximum(u, 0.0) - jnp.minimum(u_w, 0.0)) + (jnp.maximum(v, 0.0) - jnp.minimum(v_s, 0.0))
            )
            coefs[k] = (
                a_0, -0.5 * jnp.minimum(u, 0.0), 0.5 * jnp.maximum(u_w, 0.0),
                -0.5 * jnp.minimum(v, 0.0), 0.5 * jnp.maximum(v_s, 0.0),
            )
            sides[k] = jnp.where(
                lane % 2 == 0, pltpu.roll(got_w[m, k], 1, 1), pltpu.roll(got_e[m, k], LANES - 1, 1)
            )

        def advect(k, t):
            a_0, a_e, a_w, a_n, a_s = coefs[k]
            x = source[t, k]
            edge = pltpu.roll(sides[k], (LANES - 2 * t) % LANES, 1)
            x_n = jnp.where(row == ROWS - 1, got_n[m, k, t : t + 1, :], pltpu.roll(x, ROWS - 1, 0))
            x_s = jnp.where(row == 0, got_s[m, k, t : t + 1, :], pltpu.roll(x, 1, 0))
            x_e = jnp.where(lane == LANES - 1, edge, pltpu.roll(x, LANES - 1, 1))
            x_w = jnp.where(lane == 0, edge, pltpu.roll(x, 1, 1))
            return a_0 * x + (a_e * x_e + a_w * x_w) + (a_n * x_n + a_s * x_s)

        def shine(k):
            p, l = k // share, k % share
            prepare(k)
            lead = advect(k, 0)
            wet_k = (k < depth_here).astype(F32)
            tau, top = state
            tau = tau + (0.1 + 0.3 * jnp.maximum(lead, 0.0))
            below = jnp.exp(-tau)
            h_send[m, p, l] = 2.0 * wet_k * (top - below)
            light[k] = (lead, wet_k, top)
            state[:] = [tau, below]
            if k == depth - 1:
                for c in heats(m):
                    c.start()
                h_recv[m, col] = h_send[m, col]

        groups = depth // PAIR
        held = {}
        for g in range(groups + 1):
            if g < groups:
                if m:
                    wait_recv(second(g))
                levels = range(g * PAIR, (g + 1) * PAIR)
                for k in levels:
                    shine(k)
                adv = [
                    jnp.concatenate([light[k][0]] + [advect(k, t) for t in range(1, tracers)], axis=0)
                    for k in levels
                ]
                hi = [a.astype(jnp.bfloat16) for a in adv]
                lo = [(a - b.astype(F32)).astype(jnp.bfloat16) for a, b in zip(adv, hi)]
                held[g] = (adv, jnp.concatenate(hi, axis=1), jnp.concatenate(lo, axis=1))
            if g > 0:
                adv, hi, lo = held.pop(g - 1)
                r = (
                    jnp.dot(rates_hi, hi, preferred_element_type=F32)
                    + jnp.dot(rates_hi, lo, preferred_element_type=F32)
                    + jnp.dot(rates_lo, hi, preferred_element_type=F32)
                )
                for n in range(PAIR):
                    k = (g - 1) * PAIR + n
                    _, wet_k, top = light[k]
                    gain = r[:, n * LANES : (n + 1) * LANES].reshape(tracers, ROWS, LANES)
                    new = wet_k * (adv[n].reshape(tracers, ROWS, LANES) + (0.5 * top) * gain)
                    target[:, k] = new
                    if m == 0:
                        pack(1, k, new)
                    else:
                        saves[4 + k].start()
                if m == 0:
                    start(second(g - 1))

    wait_recv(first)
    for c in faces(0):
        c.wait_recv()
    tile_step(0, c_in, c_mid)
    for c in faces(1):
        c.wait_recv()
    tile_step(1, c_mid, c_out)

    for c in heats(0):
        c.wait_recv()
    for p in range(nlon):
        cols = slice(p * LANES, (p + 1) * LANES)
        t_out[:, :, cols] = t_base[:, :, cols] + 0.5 * wet_strip[:, :, cols] * h_recv[0, p]
    saves[2].start()
    wait_send(dyn)
    wait_send(first)
    for g in range(depth // PAIR):
        wait_send(second(g))
    for m in range(2):
        for c in faces(m):
            c.wait_send()
        for c in heats(m):
            c.wait_send()
    for c in heats(1):
        c.wait_recv()
    for p in range(nlon):
        h_out[:, :, p * LANES : (p + 1) * LANES] = h_recv[1, p]
    saves[3].start()
    for save in saves:
        save.wait()


def store(*refs):
    half = len(refs) // 3
    sources, results, held, (load_sem, save_sem) = refs[:half], refs[half : 2 * half], refs[2 * half : -2], refs[-2:]
    cut = sources[-1].shape[0] // CUTS
    pieces = [(i, slice(None)) for i in range(half - 1)]
    pieces = [(half - 1, slice(i * cut, (i + 1) * cut)) for i in range(CUTS)] + pieces
    loads, saves = [], []
    for n, (i, piece) in enumerate(pieces):
        loads.append(pltpu.make_async_copy(sources[i].at[piece], held[i].at[piece], load_sem.at[n]))
        saves.append(pltpu.make_async_copy(held[i].at[piece], results[i].at[piece], save_sem.at[n]))
    for load in loads:
        load.start()
    for load, save in zip(loads, saves):
        load.wait()
        save.start()
    for save in saves:
        save.wait()


def shards(sizes, u, v, t, h, c, n, r):
    tracers, depth, share, nlon, _, _ = sizes
    strip = jax.ShapeDtypeStruct(u.shape, F32)
    tile = (ROWS, LANES)
    strip_buf = pltpu.VMEM(u.shape, F32)
    dma = pltpu.SemaphoreType.DMA
    hbm = pl.BlockSpec(memory_space=pltpu.HBM)
    outs = pl.pallas_call(
        functools.partial(kernel, sizes),
        out_shape=(strip, strip, strip, strip, jax.ShapeDtypeStruct(c.shape, F32)),
        in_specs=[hbm] * 7,
        out_specs=(hbm,) * 5,
        scratch_shapes=[
            strip_buf, strip_buf, strip_buf, strip_buf,
            pltpu.VMEM(n.shape, jnp.int32), pltpu.VMEM(n.shape, jnp.int32),
            pltpu.VMEM((4, share, EXT, u.shape[2]), F32),
            pltpu.VMEM((EXT, u.shape[2]), jnp.int32),
            strip_buf, strip_buf,
            pltpu.VMEM(c.shape, F32),
            pltpu.VMEM((2, depth, tracers, LANES), F32),
            pltpu.VMEM((2, depth, tracers, LANES), F32),
            pltpu.VMEM((2, depth) + tile, F32),
            pltpu.VMEM((2, depth, tracers, LANES), F32),
            pltpu.VMEM((2, depth, tracers, LANES), F32),
            pltpu.VMEM((2, depth) + tile, F32),
            pltpu.VMEM((2, depth) + tile, F32),
            pltpu.VMEM((2, nlon, 2 * share + 2) + tile, F32),
            pltpu.VMEM((2, nlon, 2 * share + 2) + tile, F32),
            pltpu.VMEM((2, nlon, share) + tile, F32),
            pltpu.VMEM((2, nlon, share) + tile, F32),
            strip_buf, strip_buf, strip_buf, strip_buf, pltpu.VMEM(c.shape, F32),
            pltpu.VMEM(n.shape, jnp.int32), pltpu.VMEM(r.shape, F32), dma((7,)),
            strip_buf, strip_buf, strip_buf, strip_buf, pltpu.VMEM(c.shape, F32), dma((4 + c.shape[1],)),
            dma((4,)), dma((4,)), dma((4,)), dma((4,)),
            dma((4, depth)), dma((4, depth)),
            dma((2, nlon)), dma((2, nlon)), dma((2, nlon)), dma((2, nlon)),
        ],
        compiler_params=pltpu.CompilerParams(
            collective_id=0, has_side_effects=True, vmem_limit_bytes=VMEM
        ),
    )(u, v, t, h, c, n, r)
    return pl.pallas_call(
        store,
        out_shape=(strip, strip, strip, strip, jax.ShapeDtypeStruct(c.shape, F32)),
        in_specs=[hbm] * 5,
        out_specs=(hbm,) * 5,
        scratch_shapes=[strip_buf] * 4 + [pltpu.VMEM(c.shape, F32), dma((4 + CUTS,)), dma((4 + CUTS,))],
        compiler_params=pltpu.CompilerParams(vmem_limit_bytes=VMEM),
    )(*outs)


def solution(mesh):
    nlon, nrole = mesh.shape["lon"], mesh.shape["role"]
    nstrip = mesh.shape["lat"] * nrole
    strip = P("lon", ("grp", "lat", "role"), None)
    tile = P(None, None, ("grp", "lat", "role"), "lon")

    def run(u, v, t, h, c, n, r):
        sizes = (c.shape[0], c.shape[1], u.shape[0] // nlon, nlon, nrole, nstrip)
        return jax.shard_map(
            functools.partial(shards, sizes),
            mesh=mesh,
            in_specs=(strip, strip, strip, strip, tile, P(("grp", "lat", "role"), None), P()),
            out_specs=(strip, strip, strip, strip, tile),
            check_vma=False,
        )(u, v, t, h, c, n, r)

    return run
```

```python
import functools

import jax
import jax.numpy as jnp
from jax import lax
from jax.experimental import pallas as pl
from jax.experimental.pallas import tpu as pltpu
from jax.sharding import PartitionSpec as P

ROWS = 8
LANES = 128
PAD = 4
EXT = ROWS + 2 * PAD
PAIR = 2
VMEM = 64 * 1024 * 1024
CUTS = 8
F32 = jnp.float32


def east(q):
    lane = lax.broadcasted_iota(jnp.int32, q.shape, q.ndim - 1)
    return jnp.where(lane < q.shape[-1] - 1, pltpu.roll(q, q.shape[-1] - 1, q.ndim - 1), 0.0)


def west(q):
    lane = lax.broadcasted_iota(jnp.int32, q.shape, q.ndim - 1)
    return jnp.where(lane > 0, pltpu.roll(q, 1, q.ndim - 1), 0.0)


def north(q):
    return pltpu.roll(q, q.shape[-2] - 1, q.ndim - 2)


def south(q):
    return pltpu.roll(q, 1, q.ndim - 2)


def lap(q):
    return east(q) + west(q) + north(q) + south(q) - 4.0 * q


def kernel(
    sizes,
    u_hbm, v_hbm, t_hbm, h_hbm, c_hbm, n_hbm, r_hbm,
    u_dst, v_dst, t_dst, h_dst, c_dst,
    pk_n, pk_s, rc_n, rc_s, cnt_n, cnt_s, ext, ext_n, t_base, wet_strip,
    c_mid, row_lo, row_hi, col_ed, got_n, got_s, got_w, got_e,
    f_send, f_recv, h_send, h_recv,
    u_in, v_in, t_in, h_in, c_in, n_in, r_in, in_sem,
    u_out, v_out, t_out, h_out, c_out, out_sem,
    d_ssem, d_rsem, c0_ssem, c0_rsem, c1_ssem, c1_rsem, f_ssem, f_rsem, h_ssem, h_rsem,
):
    tracers, depth, share, nlon, nrole, nstrip = sizes
    width = nlon * LANES
    arrays = (
        (u_hbm, u_in), (v_hbm, v_in), (t_hbm, t_in), (h_hbm, h_in), (n_hbm, n_in), (c_hbm, c_in), (r_hbm, r_in),
    )
    loads = [pltpu.make_async_copy(a, b, in_sem.at[i]) for i, (a, b) in enumerate(arrays)]
    for load in loads:
        load.start()
    s = lax.axis_index("lat") * nrole + lax.axis_index("role")
    col = lax.axis_index("lon")
    has_n, has_s = s < nstrip - 1, s > 0
    has_e, has_w = col < nlon - 1, col > 0
    sn, ss = lax.rem(s + 1, nstrip), lax.rem(s + nstrip - 1, nstrip)
    dev_n = {"lat": sn // nrole, "role": lax.rem(sn, nrole)}
    dev_s = {"lat": ss // nrole, "role": lax.rem(ss, nrole)}
    dev_e = {"lon": lax.rem(col + 1, nlon)}
    dev_w = {"lon": lax.rem(col + nlon - 1, nlon)}

    barrier = pltpu.get_barrier_semaphore()

    def greet(dev):
        pl.semaphore_signal(barrier, inc=1, device_id=dev, device_id_type=pl.DeviceIdType.MESH)

    pl.when(has_n)(lambda: greet(dev_n))
    pl.when(has_s)(lambda: greet(dev_s))
    for d in range(1, nlon):
        greet({"lon": lax.rem(col + d, nlon)})

    def copy(src, dst, ssem, rsem, dev):
        return pltpu.make_async_remote_copy(
            src_ref=src, dst_ref=dst, send_sem=ssem, recv_sem=rsem,
            device_id=dev, device_id_type=pl.DeviceIdType.MESH,
        )

    def start(copies):
        for c, send, _ in copies:
            pl.when(send)(c.start)

    def wait_recv(copies):
        for c, _, recv in copies:
            pl.when(recv)(c.wait_recv)

    def wait_send(copies):
        for c, send, _ in copies:
            pl.when(send)(c.wait_send)

    for load in loads[:5]:
        load.wait()
    pk_n[:, 0:3, :] = v_in[:, 5:8, :]
    pk_n[:, 3:5, :] = u_in[:, 6:8, :]
    pk_n[:, 5:7, :] = t_in[:, 6:8, :]
    pk_n[:, 7:8, :] = h_in[:, 7:8, :]
    pk_s[:, 0:2, :] = u_in[:, 0:2, :]
    pk_s[:, 2:4, :] = v_in[:, 0:2, :]
    pk_s[:, 4:6, :] = t_in[:, 0:2, :]
    pk_s[:, 6:7, :] = h_in[:, 0:1, :]
    pk_s[:, 7:8, :] = h_in[:, 0:1, :]

    lane = lax.broadcasted_iota(jnp.int32, (ROWS, LANES), 1)
    row = lax.broadcasted_iota(jnp.int32, (ROWS, LANES), 0)

    def pack(m, k, x):
        row_lo[m, k] = x[:, 0, :]
        row_hi[m, k] = x[:, ROWS - 1, :]
        acc = x[0]
        for t in range(1, tracers):
            here = (lane == 2 * t - 1) | (lane == 2 * t)
            acc = jnp.where(here, pltpu.roll(x[t], 2 * t, 1), acc)
        col_ed[m, k] = acc

    dyn = [
        (copy(pk_n, rc_s, d_ssem.at[0], d_rsem.at[0], dev_n), has_n, has_s),
        (copy(pk_s, rc_n, d_ssem.at[1], d_rsem.at[1], dev_s), has_s, has_n),
        (copy(n_in, cnt_s, d_ssem.at[2], d_rsem.at[2], dev_n), has_n, has_s),
        (copy(n_in, cnt_n, d_ssem.at[3], d_rsem.at[3], dev_s), has_s, has_n),
    ]
    first = [
        (copy(row_hi.at[0], got_s.at[0], c0_ssem.at[0], c0_rsem.at[0], dev_n), has_n, has_s),
        (copy(row_lo.at[0], got_n.at[0], c0_ssem.at[1], c0_rsem.at[1], dev_s), has_s, has_n),
        (copy(col_ed.at[0], got_w.at[0], c0_ssem.at[2], c0_rsem.at[2], dev_e), has_e, has_w),
        (copy(col_ed.at[0], got_e.at[0], c0_ssem.at[3], c0_rsem.at[3], dev_w), has_w, has_e),
    ]

    def second(g):
        two = pl.ds(g * PAIR, PAIR)
        routes = (
            (row_hi, got_s, dev_n, has_n, has_s), (row_lo, got_n, dev_s, has_s, has_n),
            (col_ed, got_w, dev_e, has_e, has_w), (col_ed, got_e, dev_w, has_w, has_e),
        )
        return [
            (copy(a.at[1, two], b.at[1, two], c1_ssem.at[i, g], c1_rsem.at[i, g], dev), send, recv)
            for i, (a, b, dev, send, recv) in enumerate(routes)
        ]

    def faces(m):
        out = []
        for d in range(1, nlon):
            p = lax.rem(col + d, nlon)
            out.append(copy(f_send.at[m, p], f_recv.at[m, col], f_ssem.at[m, d], f_rsem.at[m, d], {"lon": p}))
        return out

    def heats(m):
        out = []
        for d in range(1, nlon):
            p = lax.rem(col + d, nlon)
            out.append(copy(h_send.at[m, p], h_recv.at[m, col], h_ssem.at[m, d], h_rsem.at[m, d], {"lon": p}))
        return out

    pl.semaphore_wait(barrier, nlon - 1 + jnp.minimum(s, 1) + jnp.minimum(nstrip - 1 - s, 1))
    start(dyn)
    for load in loads[5:]:
        load.wait()
    for k in range(depth):
        pack(0, k, c_in[:, k])
    start(first)

    @pl.when(jnp.logical_not(has_s))
    def _():
        rc_s[...] = jnp.zeros_like(rc_s)
        cnt_s[...] = jnp.zeros_like(cnt_s)
        got_s[...] = jnp.zeros_like(got_s)

    @pl.when(jnp.logical_not(has_n))
    def _():
        rc_n[...] = jnp.zeros_like(rc_n)
        cnt_n[...] = jnp.zeros_like(cnt_n)
        got_n[...] = jnp.zeros_like(got_n)

    @pl.when(jnp.logical_not(has_w))
    def _():
        got_w[...] = jnp.zeros_like(got_w)

    @pl.when(jnp.logical_not(has_e))
    def _():
        got_e[...] = jnp.zeros_like(got_e)

    zero = jnp.zeros((share, PAD, width), F32)
    for f in range(4):
        ext[f, :, 0:PAD, :] = zero
        ext[f, :, PAD + ROWS :, :] = zero
    ext_n[0:PAD, :] = jnp.zeros((PAD, width), jnp.int32)
    ext_n[PAD + ROWS :, :] = jnp.zeros((PAD, width), jnp.int32)
    for f, ref in enumerate((u_in, v_in, t_in, h_in)):
        ext[f, :, PAD : PAD + ROWS, :] = ref[...]
    ext_n[PAD : PAD + ROWS, :] = n_in[...]

    wait_recv(dyn)
    ext[0, :, 2:4, :] = rc_s[:, 3:5, :]
    ext[1, :, 1:4, :] = rc_s[:, 0:3, :]
    ext[2, :, 2:4, :] = rc_s[:, 5:7, :]
    ext[3, :, 3:4, :] = rc_s[:, 7:8, :]
    ext[0, :, 12:14, :] = rc_n[:, 0:2, :]
    ext[1, :, 12:14, :] = rc_n[:, 2:4, :]
    ext[2, :, 12:14, :] = rc_n[:, 4:6, :]
    ext[3, :, 12:13, :] = rc_n[:, 6:7, :]
    ext_n[2:4, :] = cnt_s[6:8, :]
    ext_n[12:14, :] = cnt_n[0:2, :]

    shape = (share, EXT, width)
    level = col * share + lax.broadcasted_iota(jnp.int32, shape, 0)
    wet = (level < ext_n[...][None]).astype(F32)
    wet_u = wet * east(wet)
    wet_v = wet * north(wet)
    spot = (s * ROWS - PAD + lax.broadcasted_iota(jnp.int32, shape, 1)).astype(F32)
    fcor = 0.3 * (2.0 * (spot + 0.5) / (nstrip * ROWS) - 1.0)

    def advance(u, v, t):
        new_u = wet_u * (u + 0.1 * lap(u) + fcor * v - 0.2 * (east(t) - t))
        new_v = wet_v * (v + 0.1 * lap(v) - fcor * u - 0.2 * (north(t) - t))
        return new_u, new_v

    def publish(m, u, v):
        for p in range(nlon):
            lo = p * LANES
            cols = slice(lo, lo + LANES)
            v_edge = jnp.zeros((ROWS, LANES), F32)
            u_edge = jnp.zeros((ROWS, LANES), F32)
            for l in range(share):
                f_send[m, p, l] = u[l, PAD : PAD + ROWS, cols]
                f_send[m, p, share + l] = v[l, PAD : PAD + ROWS, cols]
                v_edge = jnp.where(row == l, v[l, PAD - 1 : PAD, cols], v_edge)
                if p:
                    u_edge = jnp.where(lane == l, u[l, PAD : PAD + ROWS, lo - 1 : lo], u_edge)
            f_send[m, p, 2 * share] = v_edge
            f_send[m, p, 2 * share + 1] = u_edge
        for c in faces(m):
            c.start()
        f_recv[m, col] = f_send[m, col]

    u0, v0, t0 = ext[0], ext[1], ext[2]
    u1, v1 = advance(u0, v0, t0)
    publish(0, u1, v1)
    t1 = wet * (t0 + 0.1 * lap(t0) + 0.5 * ext[3])
    u2, v2 = advance(u1, v1, t1)
    publish(1, u2, v2)
    saves = [
        pltpu.make_async_copy(a, b, out_sem.at[i])
        for i, (a, b) in enumerate(((u_out, u_dst), (v_out, v_dst), (t_out, t_dst), (h_out, h_dst)))
    ]
    saves += [pltpu.make_async_copy(c_out.at[:, k], c_dst.at[:, k], out_sem.at[4 + k]) for k in range(depth)]
    u_out[...] = u2[:, PAD : PAD + ROWS, :]
    v_out[...] = v2[:, PAD : PAD + ROWS, :]
    saves[0].start()
    saves[1].start()
    t_base[...] = (wet * (t1 + 0.1 * lap(t1)))[:, PAD : PAD + ROWS, :]
    wet_strip[...] = wet[:, PAD : PAD + ROWS, :]

    wide = tracers * ROWS
    spread = (
        lax.broadcasted_iota(jnp.int32, (wide, tracers), 0) // ROWS
        == lax.broadcasted_iota(jnp.int32, (wide, tracers), 1)
    ).astype(F32)
    gather = (
        lax.broadcasted_iota(jnp.int32, (tracers, wide), 1) // ROWS
        == lax.broadcasted_iota(jnp.int32, (tracers, wide), 0)
    ).astype(F32)
    exact = lax.Precision.HIGHEST
    rates = jnp.dot(
        spread, jnp.dot(r_in[...], gather, precision=exact, preferred_element_type=F32),
        precision=exact, preferred_element_type=F32,
    )
    same_row = (
        lax.broadcasted_iota(jnp.int32, (wide, wide), 0) % ROWS
        == lax.broadcasted_iota(jnp.int32, (wide, wide), 1) % ROWS
    )
    rates = jnp.where(same_row, rates, 0.0)
    rates_hi = rates.astype(jnp.bfloat16)
    rates_lo = (rates - rates_hi.astype(F32)).astype(jnp.bfloat16)

    depth_here = n_in[:, pl.ds(pl.multiple_of(col * LANES, LANES), LANES)]

    def tile_step(m, source, target):
        coefs, sides, light = {}, {}, {}
        state = [jnp.zeros((ROWS, LANES), F32), jnp.ones((ROWS, LANES), F32)]

        def prepare(k):
            p, l = k // share, k % share
            u = f_recv[m, p, l]
            v = f_recv[m, p, share + l]
            v_s = jnp.where(row == 0, f_recv[m, p, 2 * share, l : l + 1, :], pltpu.roll(v, 1, 0))
            u_w = jnp.where(lane == 0, f_recv[m, p, 2 * share + 1, :, l : l + 1], pltpu.roll(u, 1, 1))
            a_0 = 1.0 - 0.5 * (
                (jnp.maximum(u, 0.0) - jnp.minimum(u_w, 0.0)) + (jnp.maximum(v, 0.0) - jnp.minimum(v_s, 0.0))
            )
            coefs[k] = (
                a_0, -0.5 * jnp.minimum(u, 0.0), 0.5 * jnp.maximum(u_w, 0.0),
                -0.5 * jnp.minimum(v, 0.0), 0.5 * jnp.maximum(v_s, 0.0),
            )
            sides[k] = jnp.where(
                lane % 2 == 0, pltpu.roll(got_w[m, k], 1, 1), pltpu.roll(got_e[m, k], LANES - 1, 1)
            )

        def advect(k, t):
            a_0, a_e, a_w, a_n, a_s = coefs[k]
            x = source[t, k]
            edge = pltpu.roll(sides[k], (LANES - 2 * t) % LANES, 1)
            x_n = jnp.where(row == ROWS - 1, got_n[m, k, t : t + 1, :], pltpu.roll(x, ROWS - 1, 0))
            x_s = jnp.where(row == 0, got_s[m, k, t : t + 1, :], pltpu.roll(x, 1, 0))
            x_e = jnp.where(lane == LANES - 1, edge, pltpu.roll(x, LANES - 1, 1))
            x_w = jnp.where(lane == 0, edge, pltpu.roll(x, 1, 1))
            return a_0 * x + (a_e * x_e + a_w * x_w) + (a_n * x_n + a_s * x_s)

        def shine(k):
            p, l = k // share, k % share
            prepare(k)
            lead = advect(k, 0)
            wet_k = (k < depth_here).astype(F32)
            tau, top = state
            tau = tau + (0.1 + 0.3 * jnp.maximum(lead, 0.0))
            below = jnp.exp(-tau)
            h_send[m, p, l] = 2.0 * wet_k * (top - below)
            light[k] = (lead, wet_k, top)
            state[:] = [tau, below]
            if k == depth - 1:
                for c in heats(m):
                    c.start()
                h_recv[m, col] = h_send[m, col]

        held = {}

        def fluxes(g):
            if m:
                wait_recv(second(g))
            levels = range(g * PAIR, (g + 1) * PAIR)
            for k in levels:
                shine(k)
            adv = [
                jnp.concatenate([light[k][0]] + [advect(k, t) for t in range(1, tracers)], axis=0)
                for k in levels
            ]
            hi = [a.astype(jnp.bfloat16) for a in adv]
            lo = [(a - b.astype(F32)).astype(jnp.bfloat16) for a, b in zip(adv, hi)]
            held[g] = (adv, jnp.concatenate(hi, axis=1), jnp.concatenate(lo, axis=1))

        def products(g):
            adv, hi, lo = held.pop(g)
            r = (
                jnp.dot(rates_hi, hi, preferred_element_type=F32)
                + jnp.dot(rates_hi, lo, preferred_element_type=F32)
                + jnp.dot(rates_lo, hi, preferred_element_type=F32)
            )
            for n in range(PAIR):
                k = g * PAIR + n
                _, wet_k, top = light[k]
                gain = r[:, n * LANES : (n + 1) * LANES].reshape(tracers, ROWS, LANES)
                new = wet_k * (adv[n].reshape(tracers, ROWS, LANES) + (0.5 * top) * gain)
                target[:, k] = new
                if m == 0:
                    pack(1, k, new)
                else:
                    saves[4 + k].start()
            if m == 0:
                start(second(g))

        return fluxes, products

    pairs = depth // PAIR
    parts = [tile_step(0, c_in, c_mid), tile_step(1, c_mid, c_out)]
    order = [(m, g) for m in range(2) for g in range(pairs)]
    wait_recv(first)
    for c in faces(0):
        c.wait_recv()
    for n, (m, g) in enumerate(order):
        if (m, g) == (1, 0):
            for c in faces(1):
                c.wait_recv()
        parts[m][0](g)
        if n:
            parts[order[n - 1][0]][1](order[n - 1][1])
    parts[1][1](pairs - 1)

    for c in heats(0):
        c.wait_recv()
    for p in range(nlon):
        cols = slice(p * LANES, (p + 1) * LANES)
        t_out[:, :, cols] = t_base[:, :, cols] + 0.5 * wet_strip[:, :, cols] * h_recv[0, p]
    saves[2].start()
    wait_send(dyn)
    wait_send(first)
    for g in range(depth // PAIR):
        wait_send(second(g))
    for m in range(2):
        for c in faces(m):
            c.wait_send()
        for c in heats(m):
            c.wait_send()
    for c in heats(1):
        c.wait_recv()
    for p in range(nlon):
        h_out[:, :, p * LANES : (p + 1) * LANES] = h_recv[1, p]
    saves[3].start()
    for save in saves:
        save.wait()


def store(*refs):
    half = len(refs) // 3
    sources, results, held, (load_sem, save_sem) = refs[:half], refs[half : 2 * half], refs[2 * half : -2], refs[-2:]
    cut = sources[-1].shape[0] // CUTS
    pieces = [(i, slice(None)) for i in range(half - 1)]
    pieces = [(half - 1, slice(i * cut, (i + 1) * cut)) for i in range(CUTS)] + pieces
    loads, saves = [], []
    for n, (i, piece) in enumerate(pieces):
        loads.append(pltpu.make_async_copy(sources[i].at[piece], held[i].at[piece], load_sem.at[n]))
        saves.append(pltpu.make_async_copy(held[i].at[piece], results[i].at[piece], save_sem.at[n]))
    for load in loads:
        load.start()
    for load, save in zip(loads, saves):
        load.wait()
        save.start()
    for save in saves:
        save.wait()


def shards(sizes, u, v, t, h, c, n, r):
    tracers, depth, share, nlon, _, _ = sizes
    strip = jax.ShapeDtypeStruct(u.shape, F32)
    tile = (ROWS, LANES)
    strip_buf = pltpu.VMEM(u.shape, F32)
    dma = pltpu.SemaphoreType.DMA
    hbm = pl.BlockSpec(memory_space=pltpu.HBM)
    outs = pl.pallas_call(
        functools.partial(kernel, sizes),
        out_shape=(strip, strip, strip, strip, jax.ShapeDtypeStruct(c.shape, F32)),
        in_specs=[hbm] * 7,
        out_specs=(hbm,) * 5,
        scratch_shapes=[
            strip_buf, strip_buf, strip_buf, strip_buf,
            pltpu.VMEM(n.shape, jnp.int32), pltpu.VMEM(n.shape, jnp.int32),
            pltpu.VMEM((4, share, EXT, u.shape[2]), F32),
            pltpu.VMEM((EXT, u.shape[2]), jnp.int32),
            strip_buf, strip_buf,
            pltpu.VMEM(c.shape, F32),
            pltpu.VMEM((2, depth, tracers, LANES), F32),
            pltpu.VMEM((2, depth, tracers, LANES), F32),
            pltpu.VMEM((2, depth) + tile, F32),
            pltpu.VMEM((2, depth, tracers, LANES), F32),
            pltpu.VMEM((2, depth, tracers, LANES), F32),
            pltpu.VMEM((2, depth) + tile, F32),
            pltpu.VMEM((2, depth) + tile, F32),
            pltpu.VMEM((2, nlon, 2 * share + 2) + tile, F32),
            pltpu.VMEM((2, nlon, 2 * share + 2) + tile, F32),
            pltpu.VMEM((2, nlon, share) + tile, F32),
            pltpu.VMEM((2, nlon, share) + tile, F32),
            strip_buf, strip_buf, strip_buf, strip_buf, pltpu.VMEM(c.shape, F32),
            pltpu.VMEM(n.shape, jnp.int32), pltpu.VMEM(r.shape, F32), dma((7,)),
            strip_buf, strip_buf, strip_buf, strip_buf, pltpu.VMEM(c.shape, F32), dma((4 + c.shape[1],)),
            dma((4,)), dma((4,)), dma((4,)), dma((4,)),
            dma((4, depth)), dma((4, depth)),
            dma((2, nlon)), dma((2, nlon)), dma((2, nlon)), dma((2, nlon)),
        ],
        compiler_params=pltpu.CompilerParams(
            collective_id=0, has_side_effects=True, vmem_limit_bytes=VMEM
        ),
    )(u, v, t, h, c, n, r)
    return pl.pallas_call(
        store,
        out_shape=(strip, strip, strip, strip, jax.ShapeDtypeStruct(c.shape, F32)),
        in_specs=[hbm] * 5,
        out_specs=(hbm,) * 5,
        scratch_shapes=[strip_buf] * 4 + [pltpu.VMEM(c.shape, F32), dma((4 + CUTS,)), dma((4 + CUTS,))],
        compiler_params=pltpu.CompilerParams(vmem_limit_bytes=VMEM),
    )(*outs)


def solution(mesh):
    nlon, nrole = mesh.shape["lon"], mesh.shape["role"]
    nstrip = mesh.shape["lat"] * nrole
    strip = P("lon", ("grp", "lat", "role"), None)
    tile = P(None, None, ("grp", "lat", "role"), "lon")

    def run(u, v, t, h, c, n, r):
        sizes = (c.shape[0], c.shape[1], u.shape[0] // nlon, nlon, nrole, nstrip)
        return jax.shard_map(
            functools.partial(shards, sizes),
            mesh=mesh,
            in_specs=(strip, strip, strip, strip, tile, P(("grp", "lat", "role"), None), P()),
            out_specs=(strip, strip, strip, strip, tile),
            check_vma=False,
        )(u, v, t, h, c, n, r)

    return run
```
